32 devices in a mesh: grp: 8 (over y, x, core), tp: 4 (over z).
Axes of the slice: x: 2, y: 2, z: 4, core: 2. Of those that a mesh axis runs over, the one named last changes fastest.
Arguments:
- x_rows: bfloat16 [8192, 4096], P(('grp', 'tp')), may hold values from -6 to 6
- norm_gain: float32 [4096], replicated, may hold values from 0.1 to 1.9
- w_query: bfloat16 [4096, 4096], P(None, 'tp'), may hold values from -0.25 to 0.25
- w_keyval: bfloat16 [4096, 2, 1024], P(None, None, 'tp'), may hold values from -0.09375 to 0.09375
- w_out: bfloat16 [4096, 4096], P('tp'), may hold values from -0.75 to 0.75
- prefix_cache: bfloat16 [16, 128, 2, 1024], P('grp', None, None, 'tp'), may hold values from -70 to 70, as said below
- page_table: int32 [16], replicated, may hold values from 0 to 15, each once
- request_ids: int32 [8192], replicated, may hold values from 0 to 15, never falling along the last dimension, each value on 1 to 1024 neighbouring positions
Outputs:
- attn_out: bfloat16 [8192, 4096], P(('grp', 'tp'))
The draws below stay inside these ranges and needn't reach their ends.
Inputs may be any that keep to these rules, and one draw needn't show every extreme that they name: `request_ids`: request ids never fall along the stream; each of the 16 requests has 1 to 1024 tokens, one exactly 1024. `page_table`: a permutation; physical page f belongs to group f // 2. `prefix_cache`: keys are stored already rotated for their positions.
All inputs are finite; a program needn't handle non-finite values.
Results may differ from the reference program's by a relative error of at most 0.025.
The reference program's roundings to bfloat16 on the way (of `normed`, `queries`, `keyval`, `keys_new`, `logical`, `weights` and `attn`) count: a program that leaves them out, or rounds other values in their place, can miss the bound.
Values may be sent and summed in bfloat16 or wider, within the bound.
No kernel may reach another device: no remote copies, remote signals or barrier semaphores. Data moves between devices by JAX's collectives and lax.ppermute only.
A program may use at most 128 MiB of HBM per device.

```python
import math
import jax
import jax.numpy as jnp
import numpy as np
from jax import lax

D = 4096
H = 32
KVH = 8
HD = 128
PAGE = 128
SINKS = 4
TOK_G = 1024
TOTAL = 8192
PAGES = 16
PREFIX = 2048
WINDOW = 2048
NSEG = 16
N_GRP = 8
N_TP = 4


def draw_prefix_cache(key, part):
    base_key = jax.random.fold_in(key, 11)
    shape = (PAGES, PAGE, 2, KVH * HD)
    base = jnp.clip(jax.random.normal(base_key, shape, jnp.float32), -6.0, 6.0)
    return base.astype(jnp.bfloat16)


def shard_levels(rng, extent, pieces, smallest, high):
    def one(position, shards_of):
        steps = jax.random.uniform(jax.random.fold_in(jax.random.fold_in(rng, 6), position), (shards_of,), jnp.float32, smallest / len(pieces), high / len(pieces))
        return jnp.repeat(jnp.exp(steps), extent[position] // shards_of).reshape((-1,) + (1,) * (len(extent) - position - 1))

    level = one(*pieces[0])
    for cut in pieces[1:]:
        level = level * one(*cut)
    return level


def split_up(count, total, bound, skew):
    loads = [(1 << 20) // math.isqrt(standing ** skew) + 1 for standing in range(2, count + 1)]
    surplus, given = total - bound - (count - 1), [1] * (count - 1)
    while surplus > 0:
        movable = [i for i in range(count - 1) if given[i] < bound]
        whole, budget = sum([loads[i] for i in movable]), surplus
        for i in movable:
            more = min(bound - given[i], max(1, budget * loads[i] // whole), surplus)
            given[i] = given[i] + more
            surplus = surplus - more
    return np.array([bound] + given)


def uneven(rng, number_of, total, most, lean):
    if number_of == 2:
        one = jax.random.randint(rng, (), max(1, total - most), min(most, total - 1) + 1)
        return jnp.stack([one, total - one])
    tallies = jnp.asarray(split_up(number_of, total, most, lean), jnp.int32)
    couples = (number_of - 1) // 2
    giver, taker = tallies[1:1 + 2 * couples:2], tallies[2:2 + 2 * couples:2]
    room = jnp.minimum(giver - 1, most - taker)
    moved = jax.random.randint(jax.random.fold_in(rng, 1), (couples,), 0, 1 << 20) % (room + 1)
    tallies = tallies.at[1:1 + 2 * couples:2].set(giver - moved).at[2:2 + 2 * couples:2].set(taker + moved)
    return tallies[jax.random.permutation(jax.random.fold_in(rng, 2), number_of)]


def scatter_about(own_key, shape, deviation, bound, cuts=(), kind=jnp.bfloat16):
    array = deviation * jax.random.normal(own_key, shape, jnp.float32)
    if cuts:
        array = array * shard_levels(own_key, shape, cuts, -0.22, 0.18)
    return jnp.clip(array, -bound, bound).astype(kind)


def setup_inputs(seed: int = 0) -> dict:
    key_list = jax.random.split(jax.random.key(seed), 9)
    x_rows = scatter_about(key_list[0], (TOTAL, D), 1.0, 6.0, ((0, 32),))
    norm_gain = jnp.clip(1.0 + 0.18 * jax.random.normal(key_list[1], (D,), jnp.float32), 0.1, 1.9)
    w_query = scatter_about(key_list[2], (D, H * HD), (D // 8) ** -0.5, 0.25, ((1, 4),))
    w_keyval = scatter_about(key_list[3], (D, 2, KVH * HD), D ** -0.5, 0.09375, ((2, 4),))
    w_out = scatter_about(key_list[4], (H * HD, D), (H * HD // 64) ** -0.5, 0.75, ((0, 4),))
    prefix_cache = draw_prefix_cache(jax.random.fold_in(key_list[8], 71), 0)
    page_table = jax.random.permutation(key_list[6], PAGES).astype(jnp.int32)
    request_ids = jnp.searchsorted(jnp.cumsum(uneven(key_list[7], NSEG, TOTAL, TOK_G, 2)), jnp.arange(TOTAL), side="right").astype(jnp.int32)
    return {"x_rows": x_rows, "norm_gain": norm_gain, "w_query": w_query, "w_keyval": w_keyval, "w_out": w_out, "prefix_cache": prefix_cache, "page_table": page_table, "request_ids": request_ids}


def settle(values):
    return lax.optimization_barrier(values.astype(jnp.bfloat16))

def rotate(values, positions):
    half = HD // 2
    freqs = 500000.0 ** (-jnp.arange(half, dtype=jnp.float32) * 2.0 / HD)
    angles = positions.astype(jnp.float32)[:, None] * freqs[None, :]
    cosine = jnp.cos(angles)[:, None, :]
    sine = jnp.sin(angles)[:, None, :]
    first = values[..., :half]
    second = values[..., half:]
    return jnp.concatenate([first * cosine - second * sine, second * cosine + first * sine], axis=-1)

def reference(x_rows, norm_gain, w_query, w_keyval, w_out, prefix_cache, page_table, request_ids):
    wide = x_rows.astype(jnp.float32)
    variance = lax.optimization_barrier(jnp.mean(wide * wide, axis=-1, keepdims=True)) + 1e-05
    inverse = lax.rsqrt(variance)
    normed = (wide * inverse * norm_gain).astype(jnp.bfloat16)
    labels = jnp.arange(NSEG, dtype=jnp.int32)
    counts = lax.optimization_barrier(jnp.sum((request_ids[:, None] == labels[None, :]).astype(jnp.int32), axis=0))
    starts = jnp.cumsum(counts) - counts
    stream_index = jnp.arange(TOTAL, dtype=jnp.int32)
    positions = (PREFIX + stream_index - starts[request_ids]).astype(jnp.int32)
    projected = jnp.dot(normed, w_query, preferred_element_type=jnp.float32).reshape(TOTAL, H, HD)
    queries = settle(rotate(projected, positions))
    keyval = settle(jnp.dot(normed, w_keyval.reshape(D, 2 * KVH * HD), preferred_element_type=jnp.float32))
    keyval = keyval.reshape(TOTAL, 2, KVH, HD)
    keys_new = settle(rotate(keyval[:, 0].astype(jnp.float32), positions))
    values_new = keyval[:, 1]
    logical = prefix_cache[page_table].reshape(PREFIX, 2, KVH, HD)
    cache_pos = jnp.arange(PREFIX, dtype=jnp.int32)

    def group_attend(group):
        query_start = (group * TOK_G).astype(jnp.int32)
        suffix_start = (jnp.maximum(group - 1, 0) * TOK_G).astype(jnp.int32)
        group_queries = lax.dynamic_slice_in_dim(queries, query_start, TOK_G, 0).reshape(TOK_G, KVH, H // KVH, HD)
        query_pos = lax.dynamic_slice_in_dim(positions, query_start, TOK_G, 0)
        query_seg = lax.dynamic_slice_in_dim(request_ids, query_start, TOK_G, 0)
        query_index = query_start + jnp.arange(TOK_G, dtype=jnp.int32)
        suffix_keys = lax.dynamic_slice_in_dim(keys_new, suffix_start, 2 * TOK_G, 0)
        suffix_values = lax.dynamic_slice_in_dim(values_new, suffix_start, 2 * TOK_G, 0)
        suffix_pos = lax.dynamic_slice_in_dim(positions, suffix_start, 2 * TOK_G, 0)
        suffix_seg = lax.dynamic_slice_in_dim(request_ids, suffix_start, 2 * TOK_G, 0)
        suffix_index = suffix_start + jnp.arange(2 * TOK_G, dtype=jnp.int32)
        prefix_mask = (cache_pos[None, :] <= query_pos[:, None]) & ((query_pos[:, None] - cache_pos[None, :] < WINDOW) | (cache_pos[None, :] < SINKS))
        suffix_mask = (suffix_seg[None, :] == query_seg[:, None]) & (suffix_index[None, :] <= query_index[:, None])
        suffix_mask = suffix_mask & ((query_pos[:, None] - suffix_pos[None, :] < WINDOW) | (suffix_pos[None, :] < SINKS))
        visible = jnp.concatenate([prefix_mask, suffix_mask], axis=1)
        all_keys = jnp.concatenate([logical[:, 0], suffix_keys], axis=0)
        all_values = jnp.concatenate([logical[:, 1], suffix_values], axis=0)

        def head_attend(item):
            head_queries, head_keys, head_values = item
            scores = jnp.einsum('qrd,kd->qrk', head_queries.astype(jnp.float32), head_keys.astype(jnp.float32)) * HD ** (-0.5)
            scores = jnp.where(visible[:, None, :], scores, -jnp.inf)
            highest = lax.optimization_barrier(jnp.max(scores, axis=-1, keepdims=True))
            weights = jnp.exp(scores - highest)
            total = lax.optimization_barrier(jnp.sum(weights, axis=-1, keepdims=True))
            rounded = settle(weights).astype(jnp.float32)
            return jnp.einsum('qrk,kd->qrd', rounded, head_values.astype(jnp.float32)) / total
        result = lax.map(head_attend, (jnp.moveaxis(group_queries, 1, 0), jnp.moveaxis(all_keys, 1, 0), jnp.moveaxis(all_values, 1, 0)))
        return jnp.moveaxis(result, 0, 1).reshape(TOK_G, H * HD).astype(jnp.bfloat16)
    attn = lax.map(group_attend, jnp.arange(N_GRP, dtype=jnp.int32)).reshape(TOTAL, H * HD)
    heads_dev = H // N_TP

    def add_part(running, shard):
        offset = (shard * heads_dev * HD).astype(jnp.int32)
        columns = lax.dynamic_slice_in_dim(attn, offset, heads_dev * HD, 1)
        weight_rows = lax.dynamic_slice_in_dim(w_out, offset, heads_dev * HD, 0)
        term = settle(jnp.dot(columns, weight_rows, preferred_element_type=jnp.float32)).astype(jnp.float32)
        return (running + term, None)
    running, unused = lax.scan(add_part, jnp.zeros((TOTAL, D), jnp.float32), jnp.arange(N_TP, dtype=jnp.int32))
    return running.astype(jnp.bfloat16)
```

```python
import functools
import math

import jax
import jax.numpy as jnp
from jax import lax
from jax.experimental import pallas as pl
from jax.experimental.pallas import tpu as pltpu
from jax.sharding import PartitionSpec as P

KVH = 8
HD = 128
SINKS = 4
ROWS = 256
PREFIX_STEP = 512
SUFFIX_STEP = 256
MASKED = -1e30
EXPONENT = math.log2(math.e) * HD ** (-0.5)
VMEM_LIMIT = 48 * 1024 * 1024


def parameters():
    return pltpu.CompilerParams(vmem_limit_bytes=VMEM_LIMIT)


def project_kernel(offsets, x_ref, cos_ref, sin_ref, *refs, turned):
    pieces, out_ref = refs[:-1], refs[-1]
    total = None
    for index, piece in enumerate(pieces):
        depth = piece.shape[0]
        if len(pieces) == 1:
            columns = x_ref[...]
        else:
            columns = x_ref[:, pl.ds(pl.multiple_of(offsets[index], depth), depth)]
        term = jnp.dot(columns, piece[...], preferred_element_type=jnp.float32)
        total = term if total is None else total + term

    def store(rotated):
        for head in range(out_ref.shape[1] // HD):
            where = slice(head * HD, (head + 1) * HD)
            part = total[:, where]
            if rotated:
                part = part * cos_ref[...] + pltpu.roll(part, HD // 2, 1) * sin_ref[...]
            out_ref[:, where] = part.astype(out_ref.dtype)

    pl.when(pl.program_id(0) < turned)(lambda: store(True))
    pl.when(pl.program_id(0) >= turned)(lambda: store(False))


def project(x, pieces, offsets, cosine, sine, turned_columns):
    rows, width = x.shape
    columns = pieces[0].shape[1]
    tile = min(256, columns)

    def whole(*unused):
        return (0, 0)

    return pl.pallas_call(
        functools.partial(project_kernel, turned=turned_columns // tile),
        out_shape=jax.ShapeDtypeStruct((rows, columns), jnp.bfloat16),
        grid_spec=pltpu.PrefetchScalarGridSpec(
            num_scalar_prefetch=1,
            grid=(columns // tile,),
            in_specs=[
                pl.BlockSpec((rows, width), whole),
                pl.BlockSpec((rows, HD), whole),
                pl.BlockSpec((rows, HD), whole),
            ]
            + [pl.BlockSpec((piece.shape[0], tile), lambda j, *_: (0, j)) for piece in pieces],
            out_specs=pl.BlockSpec((rows, tile), lambda j, *_: (0, j)),
        ),
        compiler_params=parameters(),
        cost_estimate=pl.CostEstimate(
            flops=2 * rows * width * columns,
            bytes_accessed=2 * (rows * width + width * columns + rows * columns),
            transcendentals=0,
        ),
        name="project",
    )(offsets, x, cosine, sine, *pieces)


def attend_kernel(
    page_rows, bounds, q_ref, row_ref, pk_ref, pv_ref, *refs, window, spans, page_len, share
):
    suffix_refs = refs[: 2 * spans]
    out_ref, keys, values, highest, total = refs[2 * spans :]
    block = pl.program_id(1)
    prefix_len = pk_ref.shape[0]

    @pl.when(block == 0)
    def fill():
        values[:, HD:] = jnp.ones_like(values[:, HD:])
        for page in range(prefix_len // page_len):
            source = pl.ds(pl.multiple_of(page_rows[page], page_len), page_len)
            target = slice(page * page_len, (page + 1) * page_len)
            keys[target, :] = pk_ref[source, :]
            values[target, :HD] = pv_ref[source, :]
        base = prefix_len
        for span in range(spans):
            key_ref, value_ref = suffix_refs[2 * span : 2 * span + 2]
            size = key_ref.shape[0]
            keys[base : base + size, :] = key_ref[...]
            values[base : base + size, :HD] = value_ref[...]
            base += size

    highest[...] = jnp.full_like(highest, MASKED)
    total[...] = jnp.zeros_like(total)

    def step(base, size, visible):
        for head in range(share):
            queries = q_ref[:, head * HD : (head + 1) * HD]
            scores = lax.dot_general(
                queries,
                keys[pl.ds(base, size), :],
                (((1,), (1,)), ((), ())),
                preferred_element_type=jnp.float32,
            )
            if visible is not None:
                scores = jnp.where(visible, scores, MASKED)
            before = highest[head]
            after = jnp.maximum(before, jnp.max(scores, axis=1, keepdims=True))
            highest[head] = after
            spread = jnp.concatenate([after] * (size // HD), axis=1)
            weights = jnp.exp2((scores - spread) * EXPONENT)
            factor = jnp.exp2((before - after) * EXPONENT)
            total[head] = total[head] * jnp.concatenate([factor, factor], axis=1) + jnp.dot(
                weights.astype(jnp.bfloat16),
                values[pl.ds(base, size), :],
                preferred_element_type=jnp.float32,
            )

    behind_min, behind_max = bounds[4 * block], bounds[4 * block + 1]
    first_min, own_max = bounds[4 * block + 2], bounds[4 * block + 3]
    rows = q_ref.shape[0]

    def prefix_step(index, carry):
        base = pl.multiple_of(index * PREFIX_STEP, PREFIX_STEP)
        last = base + PREFIX_STEP - 1
        unmasked = (base > behind_max) & (last <= behind_min + window)
        unseen = (last <= behind_min) & (base >= SINKS)

        @pl.when(unmasked)
        def plain():
            step(base, PREFIX_STEP, None)

        @pl.when(jnp.logical_not(unmasked | unseen))
        def masked():
            behind = row_ref[:, 0:1]
            place = base + lax.broadcasted_iota(jnp.int32, (rows, PREFIX_STEP), 1)
            visible = ((place > behind) | (place < SINKS)) & (place <= behind + window)
            step(base, PREFIX_STEP, visible)

        return carry

    lax.fori_loop(0, prefix_len // PREFIX_STEP, prefix_step, 0)

    def suffix_step(index, carry):
        base = pl.multiple_of(index * SUFFIX_STEP, SUFFIX_STEP)
        place = base + lax.broadcasted_iota(jnp.int32, (rows, SUFFIX_STEP), 1)
        visible = (place >= row_ref[:, 1:2]) & (place <= row_ref[:, 2:3])
        step(pl.multiple_of(prefix_len + base, SUFFIX_STEP), SUFFIX_STEP, visible)
        return carry

    lax.fori_loop(first_min // SUFFIX_STEP, own_max // SUFFIX_STEP + 1, suffix_step, 0)
    for head in range(share):
        out_ref[:, head * HD : (head + 1) * HD] = (
            total[head][:, :HD] / total[head][:, HD:]
        ).astype(out_ref.dtype)


def attend(queries, row_info, bounds, prefix, page_rows, page_len, suffix, window):
    rows = queries.shape[0]
    kv_heads = prefix.shape[1] // (2 * HD)
    share = queries.shape[1] // (kv_heads * HD)
    prefix_len = prefix.shape[0]
    count = prefix_len + sum(part.shape[0] for part in suffix)

    def key_of(size):
        return pl.BlockSpec((size, HD), lambda h, i, *_: (0, h))

    def value_of(size):
        return pl.BlockSpec((size, HD), lambda h, i, *_: (0, kv_heads + h))

    specs = [
        pl.BlockSpec((ROWS, share * HD), lambda h, i, *_: (i, h)),
        pl.BlockSpec((ROWS, HD), lambda h, i, *_: (i, 0)),
        key_of(prefix_len),
        value_of(prefix_len),
    ]
    operands = [queries, row_info, prefix, prefix]
    for part in suffix:
        specs += [key_of(part.shape[0]), value_of(part.shape[0])]
        operands += [part, part]
    return pl.pallas_call(
        functools.partial(
            attend_kernel, window=window, spans=len(suffix), page_len=page_len, share=share
        ),
        out_shape=jax.ShapeDtypeStruct(queries.shape, jnp.bfloat16),
        grid_spec=pltpu.PrefetchScalarGridSpec(
            num_scalar_prefetch=2,
            grid=(kv_heads, rows // ROWS),
            in_specs=specs,
            out_specs=pl.BlockSpec((ROWS, share * HD), lambda h, i, *_: (i, h)),
            scratch_shapes=[
                pltpu.VMEM((count, HD), jnp.bfloat16),
                pltpu.VMEM((count, 2 * HD), jnp.bfloat16),
                pltpu.VMEM((share, ROWS, HD), jnp.float32),
                pltpu.VMEM((share, ROWS, 2 * HD), jnp.float32),
            ],
        ),
        compiler_params=parameters(),
        cost_estimate=pl.CostEstimate(
            flops=8 * rows * queries.shape[1] * (prefix_len + prefix_len // 4),
            bytes_accessed=2 * (2 * queries.size + 2 * kv_heads * HD * count),
            transcendentals=rows * queries.shape[1] // HD * prefix_len,
        ),
        name="attend",
    )(page_rows, bounds, *operands)


def outward_kernel(offsets, *refs, parts):
    out_ref, full = refs[-2:]
    attn_refs, weights = refs[: len(parts)], refs[len(parts) : -2]
    total = None
    at = 0
    for attn, count in zip(attn_refs, parts):
        if count == 1:
            weight = weights[at][...]
        else:
            for index in range(count):
                piece = weights[at + index]
                depth = piece.shape[0]
                where = pl.ds(pl.multiple_of(offsets[index], depth), depth)
                full[where, :] = piece[...]
            weight = full[...]
        at += count
        term = jnp.dot(attn[...], weight, preferred_element_type=jnp.float32)
        total = term if total is None else total + term
    out_ref[...] = total.astype(out_ref.dtype)


def outward(pairs, offsets):
    rows = pairs[0][0].shape[0]
    columns = pairs[0][1][0].shape[1]
    tile = min(512, columns)
    depth = pairs[-1][0].shape[1]
    attns = [attn for attn, unused in pairs]
    pieces = [piece for unused, stack in pairs for piece in stack]
    return pl.pallas_call(
        functools.partial(outward_kernel, parts=tuple(len(stack) for unused, stack in pairs)),
        out_shape=jax.ShapeDtypeStruct((rows, columns), jnp.bfloat16),
        grid_spec=pltpu.PrefetchScalarGridSpec(
            num_scalar_prefetch=1,
            grid=(columns // tile,),
            in_specs=[pl.BlockSpec(attn.shape, lambda j, *_: (0, 0)) for attn in attns]
            + [pl.BlockSpec((piece.shape[0], tile), lambda j, *_: (0, j)) for piece in pieces],
            out_specs=pl.BlockSpec((rows, tile), lambda j, *_: (0, j)),
            scratch_shapes=[pltpu.VMEM((depth, tile), jnp.bfloat16)],
        ),
        compiler_params=parameters(),
        cost_estimate=pl.CostEstimate(
            flops=2 * rows * columns * depth * len(pairs),
            bytes_accessed=2 * columns * (rows + depth * len(pairs)),
            transcendentals=0,
        ),
        name="outward",
    )(offsets, *attns, *pieces)


def rotation(positions):
    half = HD // 2
    freqs = 500000.0 ** (-jnp.arange(half, dtype=jnp.float32) * 2.0 / HD)
    angles = positions.astype(jnp.float32)[:, None] * freqs[None, :]
    cosine, sine = jnp.cos(angles), jnp.sin(angles)
    return jnp.concatenate([cosine, cosine], axis=1), jnp.concatenate([-sine, sine], axis=1)


def block_bounds(behind, first, own):
    def blocks(array):
        return array.reshape(-1, ROWS)

    return jnp.stack(
        [
            blocks(behind).min(axis=1),
            blocks(behind).max(axis=1),
            blocks(first).min(axis=1),
            blocks(own).max(axis=1),
        ],
        axis=1,
    ).reshape(-1).astype(jnp.int32)


def row_table(behind, first, own):
    rows = behind.shape[0]
    table = jnp.stack([behind, first, own], axis=1).astype(jnp.int32)
    return jnp.concatenate([table, jnp.zeros((rows, HD - 3), jnp.int32)], axis=1)


def normalize(x_rows, norm_gain):
    wide = x_rows.astype(jnp.float32)
    variance = jnp.mean(wide * wide, axis=-1, keepdims=True) + 1e-05
    return (wide * lax.rsqrt(variance) * norm_gain).astype(jnp.bfloat16)


def first_of_request(request_ids, wanted, count):
    labels = jnp.arange(count, dtype=jnp.int32)
    counts = jnp.sum((request_ids[:, None] == labels[None, :]).astype(jnp.int32), axis=0)
    starts = jnp.cumsum(counts) - counts
    match = wanted[:, None] == labels[None, :]
    return jnp.sum(jnp.where(match, starts[None, :], 0), axis=1)


def join_pair(lower, mine, peer):
    return jnp.where(
        lower, jnp.concatenate([mine, peer], axis=2), jnp.concatenate([peer, mine], axis=2)
    )


def swapped(block, axis, apart):
    route = [(i, i ^ 1 << apart) for i in range(lax.axis_size(axis))]
    return lax.ppermute(block, axis, route)


def shifted(block, axis, distance):
    route = [(i, i + distance) for i in range(lax.axis_size(axis) - distance)]
    return lax.ppermute(block, axis, route)


def by_heads(x_rows, norm_gain, w_query, w_keyval, w_out, prefix_cache, page_table, request_ids):
    tp_size = lax.axis_size("tp")
    grp_size = lax.axis_size("grp")
    tp_index = lax.axis_index("tp")
    grp_index = lax.axis_index("grp")
    tok_group = x_rows.shape[0] * tp_size
    kv_cols = w_keyval.shape[2]
    kv_need = max(HD, HD * KVH // tp_size)
    pages_dev, page_len = prefix_cache.shape[:2]
    prefix_len = pages_dev * grp_size * page_len
    pair_bits = (kv_need // kv_cols).bit_length() - 1
    no_offsets = jnp.zeros((1,), jnp.int32)

    normed = normalize(x_rows, norm_gain)
    tokens = lax.all_gather(normed, "tp", axis=0, tiled=True)
    group_start = grp_index * tok_group
    token_index = group_start + jnp.arange(tok_group, dtype=jnp.int32)
    own_seg = lax.dynamic_slice_in_dim(request_ids, group_start, tok_group, 0)
    own_first = first_of_request(request_ids, own_seg, 2 * grp_size)
    own_pos = prefix_len + token_index - own_first
    cosine, sine = rotation(own_pos)
    queries = project(tokens, [w_query], no_offsets, cosine, sine, w_query.shape[1])
    kv_weight = w_keyval.reshape(w_keyval.shape[0], 2 * kv_cols)
    cache = prefix_cache.reshape(pages_dev * page_len, 2, kv_cols)
    if pair_bits == 0:
        own = project(tokens, [kv_weight], no_offsets, cosine, sine, kv_cols)
    else:
        keyval = jnp.dot(tokens, kv_weight, preferred_element_type=jnp.float32)
        keyval = keyval.astype(jnp.bfloat16).reshape(tok_group, 2, kv_cols)
        for bit_num in range(pair_bits):
            lower = tp_index >> bit_num & 1 == 0
            keyval = join_pair(lower, keyval, swapped(keyval, "tp", bit_num))
            cache = join_pair(lower, cache, swapped(cache, "tp", bit_num))
        keys = keyval[:, 0].astype(jnp.float32).reshape(tok_group, -1, HD)
        keys = keys * cosine[:, None] + jnp.roll(keys, HD // 2, axis=2) * sine[:, None]
        keys = keys.reshape(tok_group, kv_need).astype(jnp.bfloat16)
        own = jnp.concatenate([keys, keyval[:, 1]], axis=1)
    before = shifted(own, "grp", 1)
    cache = cache.reshape(pages_dev * page_len, 2 * kv_need)
    prefix = lax.all_gather(cache, "grp", axis=0, tiled=True)
    behind = own_pos - prefix_len
    place = tok_group + jnp.arange(tok_group, dtype=jnp.int32)
    first = jnp.maximum(own_first - group_start + tok_group, place - prefix_len + 1)
    attn = attend(
        queries,
        row_table(behind, first, place),
        block_bounds(behind, first, place),
        prefix,
        page_table * page_len,
        page_len,
        [before, own],
        prefix_len,
    )
    return lax.psum_scatter(
        outward([(attn, [w_out])], no_offsets), "tp", scatter_dimension=0, tiled=True
    )


def solution(mesh):
    placed = (
        P(("grp", "tp"), None),
        P(),
        P(None, "tp"),
        P(None, None, "tp"),
        P("tp", None),
        P("grp", None, None, "tp"),
        P(),
        P(),
    )
    return jax.shard_map(
        by_heads, mesh=mesh, in_specs=placed, out_specs=P(("grp", "tp"), None), check_vma=False
    )
```

```python
import functools
import math

import jax
import jax.numpy as jnp
from jax import lax
from jax.experimental import pallas as pl
from jax.experimental.pallas import tpu as pltpu
from jax.sharding import PartitionSpec as P

KVH = 8
HD = 128
SINKS = 4
ROWS = 256
PREFIX_STEP = 512
SUFFIX_STEP = 256
MASKED = -1e30
EXPONENT = math.log2(math.e) * HD ** (-0.5)
VMEM_LIMIT = 48 * 1024 * 1024


def parameters():
    return pltpu.CompilerParams(vmem_limit_bytes=VMEM_LIMIT)


def project_kernel(offsets, x_ref, cos_ref, sin_ref, *refs, turned):
    pieces, out_ref = refs[:-1], refs[-1]
    total = None
    for index, piece in enumerate(pieces):
        depth = piece.shape[0]
        if len(pieces) == 1:
            columns = x_ref[...]
        else:
            columns = x_ref[:, pl.ds(pl.multiple_of(offsets[index], depth), depth)]
        term = jnp.dot(columns, piece[...], preferred_element_type=jnp.float32)
        total = term if total is None else total + term

    def store(rotated):
        for head in range(out_ref.shape[1] // HD):
            where = slice(head * HD, (head + 1) * HD)
            part = total[:, where]
            if rotated:
                part = part * cos_ref[...] + pltpu.roll(part, HD // 2, 1) * sin_ref[...]
            out_ref[:, where] = part.astype(out_ref.dtype)

    pl.when(pl.program_id(0) < turned)(lambda: store(True))
    pl.when(pl.program_id(0) >= turned)(lambda: store(False))


def project(x, pieces, offsets, cosine, sine, turned_columns):
    rows, width = x.shape
    columns = pieces[0].shape[1]
    tile = min(256, columns)

    def whole(*unused):
        return (0, 0)

    return pl.pallas_call(
        functools.partial(project_kernel, turned=turned_columns // tile),
        out_shape=jax.ShapeDtypeStruct((rows, columns), jnp.bfloat16),
        grid_spec=pltpu.PrefetchScalarGridSpec(
            num_scalar_prefetch=1,
            grid=(columns // tile,),
            in_specs=[
                pl.BlockSpec((rows, width), whole),
                pl.BlockSpec((rows, HD), whole),
                pl.BlockSpec((rows, HD), whole),
            ]
            + [pl.BlockSpec((piece.shape[0], tile), lambda j, *_: (0, j)) for piece in pieces],
            out_specs=pl.BlockSpec((rows, tile), lambda j, *_: (0, j)),
        ),
        compiler_params=parameters(),
        cost_estimate=pl.CostEstimate(
            flops=2 * rows * width * columns,
            bytes_accessed=2 * (rows * width + width * columns + rows * columns),
            transcendentals=0,
        ),
        name="project",
    )(offsets, x, cosine, sine, *pieces)


def attend_kernel(
    page_rows, bounds, q_ref, row_ref, pk_ref, pv_ref, *refs, window, spans, page_len, share
):
    suffix_refs = refs[: 2 * spans]
    out_ref, keys, values, highest, total = refs[2 * spans :]
    block = pl.program_id(1)
    prefix_len = pk_ref.shape[0]

    @pl.when(block == 0)
    def fill():
        values[:, HD:] = jnp.ones_like(values[:, HD:])
        for page in range(prefix_len // page_len):
            source = pl.ds(pl.multiple_of(page_rows[page], page_len), page_len)
            target = slice(page * page_len, (page + 1) * page_len)
            keys[target, :] = pk_ref[source, :]
            values[target, :HD] = pv_ref[source, :]
        base = prefix_len
        for span in range(spans):
            key_ref, value_ref = suffix_refs[2 * span : 2 * span + 2]
            size = key_ref.shape[0]
            keys[base : base + size, :] = key_ref[...]
            values[base : base + size, :HD] = value_ref[...]
            base += size

    highest[...] = jnp.full_like(highest, MASKED)
    total[...] = jnp.zeros_like(total)

    def step(base, size, visible):
        for head in range(share):
            queries = q_ref[:, head * HD : (head + 1) * HD]
            scores = lax.dot_general(
                queries,
                keys[pl.ds(base, size), :],
                (((1,), (1,)), ((), ())),
                preferred_element_type=jnp.float32,
            )
            if visible is not None:
                scores = jnp.where(visible, scores, MASKED)
            before = highest[head]
            after = jnp.maximum(before, jnp.max(scores, axis=1, keepdims=True))
            highest[head] = after
            spread = jnp.concatenate([after] * (size // HD), axis=1)
            weights = jnp.exp2((scores - spread) * EXPONENT)
            factor = jnp.exp2((before - after) * EXPONENT)
            total[head] = total[head] * jnp.concatenate([factor, factor], axis=1) + jnp.dot(
                weights.astype(jnp.bfloat16),
                values[pl.ds(base, size), :],
                preferred_element_type=jnp.float32,
            )

    behind_min, behind_max = bounds[4 * block], bounds[4 * block + 1]
    first_min, own_max = bounds[4 * block + 2], bounds[4 * block + 3]
    rows = q_ref.shape[0]

    def prefix_step(index, carry):
        base = pl.multiple_of(index * PREFIX_STEP, PREFIX_STEP)
        last = base + PREFIX_STEP - 1
        unmasked = (base > behind_max) & (last <= behind_min + window)
        unseen = (last <= behind_min) & (base >= SINKS)

        @pl.when(unmasked)
        def plain():
            step(base, PREFIX_STEP, None)

        @pl.when(jnp.logical_not(unmasked | unseen))
        def masked():
            behind = row_ref[:, 0:1]
            place = base + lax.broadcasted_iota(jnp.int32, (rows, PREFIX_STEP), 1)
            visible = ((place > behind) | (place < SINKS)) & (place <= behind + window)
            step(base, PREFIX_STEP, visible)

        return carry

    lax.fori_loop(0, prefix_len // PREFIX_STEP, prefix_step, 0)

    def suffix_step(index, carry):
        base = pl.multiple_of(index * SUFFIX_STEP, SUFFIX_STEP)
        place = base + lax.broadcasted_iota(jnp.int32, (rows, SUFFIX_STEP), 1)
        visible = (place >= row_ref[:, 1:2]) & (place <= row_ref[:, 2:3])
        step(pl.multiple_of(prefix_len + base, SUFFIX_STEP), SUFFIX_STEP, visible)
        return carry

    lax.fori_loop(first_min // SUFFIX_STEP, own_max // SUFFIX_STEP + 1, suffix_step, 0)
    for head in range(share):
        out_ref[:, head * HD : (head + 1) * HD] = (
            total[head][:, :HD] / total[head][:, HD:]
        ).astype(out_ref.dtype)


def attend(
    queries, row_info, bounds, prefix, page_rows, page_len, suffix, window, prefix_column=0
):
    rows = queries.shape[0]
    kv_heads = suffix[0].shape[1] // (2 * HD)
    skip = prefix_column // HD
    share = queries.shape[1] // (kv_heads * HD)
    prefix_len = prefix.shape[0]
    count = prefix_len + sum(part.shape[0] for part in suffix)

    def key_of(size, at=0):
        return pl.BlockSpec((size, HD), lambda h, i, *_: (0, at + h))

    def value_of(size, at=0):
        return pl.BlockSpec((size, HD), lambda h, i, *_: (0, at + kv_heads + h))

    specs = [
        pl.BlockSpec((ROWS, share * HD), lambda h, i, *_: (i, h)),
        pl.BlockSpec((ROWS, HD), lambda h, i, *_: (i, 0)),
        key_of(prefix_len, skip),
        value_of(prefix_len, skip),
    ]
    operands = [queries, row_info, prefix, prefix]
    for part in suffix:
        specs += [key_of(part.shape[0]), value_of(part.shape[0])]
        operands += [part, part]
    return pl.pallas_call(
        functools.partial(
            attend_kernel, window=window, spans=len(suffix), page_len=page_len, share=share
        ),
        out_shape=jax.ShapeDtypeStruct(queries.shape, jnp.bfloat16),
        grid_spec=pltpu.PrefetchScalarGridSpec(
            num_scalar_prefetch=2,
            grid=(kv_heads, rows // ROWS),
            in_specs=specs,
            out_specs=pl.BlockSpec((ROWS, share * HD), lambda h, i, *_: (i, h)),
            scratch_shapes=[
                pltpu.VMEM((count, HD), jnp.bfloat16),
                pltpu.VMEM((count, 2 * HD), jnp.bfloat16),
                pltpu.VMEM((share, ROWS, HD), jnp.float32),
                pltpu.VMEM((share, ROWS, 2 * HD), jnp.float32),
            ],
        ),
        compiler_params=parameters(),
        cost_estimate=pl.CostEstimate(
            flops=8 * rows * queries.shape[1] * (prefix_len + prefix_len // 4),
            bytes_accessed=2 * (2 * queries.size + 2 * kv_heads * HD * count),
            transcendentals=rows * queries.shape[1] // HD * prefix_len,
        ),
        name="attend",
    )(page_rows, bounds, *operands)


def outward_kernel(offsets, *refs, parts):
    out_ref, full = refs[-2:]
    attn_refs, weights = refs[: len(parts)], refs[len(parts) : -2]
    total = None
    at = 0
    for attn, count in zip(attn_refs, parts):
        if count == 1:
            weight = weights[at][...]
        else:
            for index in range(count):
                piece = weights[at + index]
                depth = piece.shape[0]
                where = pl.ds(pl.multiple_of(offsets[index], depth), depth)
                full[where, :] = piece[...]
            weight = full[...]
        at += count
        term = jnp.dot(attn[...], weight, preferred_element_type=jnp.float32)
        total = term if total is None else total + term
    out_ref[...] = total.astype(out_ref.dtype)


def outward(pairs, offsets):
    rows = pairs[0][0].shape[0]
    columns = pairs[0][1][0].shape[1]
    tile = min(512, columns)
    depth = pairs[-1][0].shape[1]
    attns = [attn for attn, unused in pairs]
    pieces = [piece for unused, stack in pairs for piece in stack]
    return pl.pallas_call(
        functools.partial(outward_kernel, parts=tuple(len(stack) for unused, stack in pairs)),
        out_shape=jax.ShapeDtypeStruct((rows, columns), jnp.bfloat16),
        grid_spec=pltpu.PrefetchScalarGridSpec(
            num_scalar_prefetch=1,
            grid=(columns // tile,),
            in_specs=[pl.BlockSpec(attn.shape, lambda j, *_: (0, 0)) for attn in attns]
            + [pl.BlockSpec((piece.shape[0], tile), lambda j, *_: (0, j)) for piece in pieces],
            out_specs=pl.BlockSpec((rows, tile), lambda j, *_: (0, j)),
            scratch_shapes=[pltpu.VMEM((depth, tile), jnp.bfloat16)],
        ),
        compiler_params=parameters(),
        cost_estimate=pl.CostEstimate(
            flops=2 * rows * columns * depth * len(pairs),
            bytes_accessed=2 * columns * (rows + depth * len(pairs)),
            transcendentals=0,
        ),
        name="outward",
    )(offsets, *attns, *pieces)


def rotation(positions):
    half = HD // 2
    freqs = 500000.0 ** (-jnp.arange(half, dtype=jnp.float32) * 2.0 / HD)
    angles = positions.astype(jnp.float32)[:, None] * freqs[None, :]
    cosine, sine = jnp.cos(angles), jnp.sin(angles)
    return jnp.concatenate([cosine, cosine], axis=1), jnp.concatenate([-sine, sine], axis=1)


def block_bounds(behind, first, own):
    def blocks(array):
        return array.reshape(-1, ROWS)

    return jnp.stack(
        [
            blocks(behind).min(axis=1),
            blocks(behind).max(axis=1),
            blocks(first).min(axis=1),
            blocks(own).max(axis=1),
        ],
        axis=1,
    ).reshape(-1).astype(jnp.int32)


def row_table(behind, first, own):
    rows = behind.shape[0]
    table = jnp.stack([behind, first, own], axis=1).astype(jnp.int32)
    return jnp.concatenate([table, jnp.zeros((rows, HD - 3), jnp.int32)], axis=1)


def normalize(x_rows, norm_gain):
    wide = x_rows.astype(jnp.float32)
    variance = jnp.mean(wide * wide, axis=-1, keepdims=True) + 1e-05
    return (wide * lax.rsqrt(variance) * norm_gain).astype(jnp.bfloat16)


def first_of_request(request_ids, wanted, count):
    labels = jnp.arange(count, dtype=jnp.int32)
    counts = jnp.sum((request_ids[:, None] == labels[None, :]).astype(jnp.int32), axis=0)
    starts = jnp.cumsum(counts) - counts
    match = wanted[:, None] == labels[None, :]
    return jnp.sum(jnp.where(match, starts[None, :], 0), axis=1)


def join_pair(lower, mine, peer):
    return jnp.where(
        lower, jnp.concatenate([mine, peer], axis=2), jnp.concatenate([peer, mine], axis=2)
    )


def swapped(block, axis, apart):
    route = [(i, i ^ 1 << apart) for i in range(lax.axis_size(axis))]
    return lax.ppermute(block, axis, route)


def shifted(block, axis, distance):
    route = [(i, i + distance) for i in range(lax.axis_size(axis) - distance)]
    return lax.ppermute(block, axis, route)


def by_heads(x_rows, norm_gain, w_query, w_keyval, w_out, prefix_cache, page_table, request_ids):
    tp_size = lax.axis_size("tp")
    grp_size = lax.axis_size("grp")
    tp_index = lax.axis_index("tp")
    grp_index = lax.axis_index("grp")
    tok_group = x_rows.shape[0] * tp_size
    kv_cols = w_keyval.shape[2]
    kv_need = max(HD, HD * KVH // tp_size)
    pages_dev, page_len = prefix_cache.shape[:2]
    prefix_len = pages_dev * grp_size * page_len
    pair_bits = (kv_need // kv_cols).bit_length() - 1
    no_offsets = jnp.zeros((1,), jnp.int32)

    normed = normalize(x_rows, norm_gain)
    tokens = lax.all_gather(normed, "tp", axis=0, tiled=True)
    group_start = grp_index * tok_group
    token_index = group_start + jnp.arange(tok_group, dtype=jnp.int32)
    own_seg = lax.dynamic_slice_in_dim(request_ids, group_start, tok_group, 0)
    own_first = first_of_request(request_ids, own_seg, 2 * grp_size)
    own_pos = prefix_len + token_index - own_first
    cosine, sine = rotation(own_pos)
    queries = project(tokens, [w_query], no_offsets, cosine, sine, w_query.shape[1])
    kv_weight = w_keyval.reshape(w_keyval.shape[0], 2 * kv_cols)
    cache = prefix_cache.reshape(pages_dev * page_len, 2, kv_cols)
    if pair_bits == 0:
        own = project(tokens, [kv_weight], no_offsets, cosine, sine, kv_cols)
    else:
        keyval = jnp.dot(tokens, kv_weight, preferred_element_type=jnp.float32)
        keyval = keyval.astype(jnp.bfloat16).reshape(tok_group, 2, kv_cols)
        for bit_num in range(pair_bits):
            lower = tp_index >> bit_num & 1 == 0
            keyval = join_pair(lower, keyval, swapped(keyval, "tp", bit_num))
            cache = join_pair(lower, cache, swapped(cache, "tp", bit_num))
        keys = keyval[:, 0].astype(jnp.float32).reshape(tok_group, -1, HD)
        keys = keys * cosine[:, None] + jnp.roll(keys, HD // 2, axis=2) * sine[:, None]
        keys = keys.reshape(tok_group, kv_need).astype(jnp.bfloat16)
        own = jnp.concatenate([keys, keyval[:, 1]], axis=1)
    before = shifted(own, "grp", 1)
    cache = cache.reshape(pages_dev * page_len, 2 * kv_need)
    prefix = lax.all_gather(cache, "grp", axis=0, tiled=True)
    behind = own_pos - prefix_len
    place = tok_group + jnp.arange(tok_group, dtype=jnp.int32)
    first = own_first - group_start + tok_group
    first = jnp.maximum(jnp.maximum(first, place - prefix_len + 1), 0)
    attn = attend(
        queries,
        row_table(behind, first, place),
        block_bounds(behind, first, place),
        prefix,
        page_table * page_len,
        page_len,
        [before, own],
        prefix_len,
    )
    return lax.psum_scatter(
        outward([(attn, [w_out])], no_offsets), "tp", scatter_dimension=0, tiled=True
    )


def by_pairs(x_rows, norm_gain, w_query, w_keyval, w_out, prefix_cache, page_table, request_ids):
    grp_size = lax.axis_size("grp")
    tp_size = lax.axis_size("tp")
    grp_index = lax.axis_index("grp")
    tp_index = lax.axis_index("tp")
    rows, width = x_rows.shape
    kv_cols = w_keyval.shape[2]
    pages_dev, page_len = prefix_cache.shape[:2]
    prefix_len = pages_dev * grp_size * page_len
    half = 2 * rows
    no_offsets = jnp.zeros((1,), jnp.int32)
    owners = grp_index ^ jnp.arange(grp_size, dtype=jnp.int32)

    def across(block, distance):
        return lax.ppermute(block, "tp", [(i, i ^ distance) for i in range(tp_size)])

    def within(block, distance):
        return lax.ppermute(block, "grp", [(i, i ^ distance) for i in range(grp_size)])

    def spread(block):
        blocks = [block] + [within(block, distance) for distance in range(2, grp_size, 2)]
        return [piece for block in blocks for piece in (block, within(block, 1))]

    def share_of(weight):
        part = weight.shape[0] // grp_size
        return lax.dynamic_slice_in_dim(weight, grp_index * part, part, 0)

    def later(block, by):
        route = []
        for place in range(2 * grp_size - by):
            target = place + by
            for side in range(2):
                route.append(
                    (place // 2 * tp_size + place % 2 * 2 + side, target // 2 * tp_size + target % 2 * 2 + side)
                )
        return lax.ppermute(block, ("grp", "tp"), route)

    far_cache = across(prefix_cache.reshape(pages_dev * page_len, 2 * kv_cols), 2)
    far_keyval = across(share_of(w_keyval).reshape(width // grp_size, 2 * kv_cols), 2)
    normed = normalize(x_rows, norm_gain)
    peer = across(normed, 1)
    far_query = across(share_of(w_query), 2)
    far_keyval = spread(far_keyval)
    near_cache = prefix_cache.reshape(pages_dev * page_len, 2 * kv_cols)
    prefix = jnp.concatenate(
        spread(jnp.concatenate([near_cache, far_cache], axis=1)), axis=0
    )
    far_query = spread(far_query)
    far_out = spread(across(share_of(w_out), 2))

    half_start = grp_index * rows * tp_size + tp_index // 2 * half

    def table_of(plane):
        place = half + half + plane % 2 * rows + jnp.arange(rows, dtype=jnp.int32)
        index = half_start - 2 * half + place
        segments = lax.dynamic_slice_in_dim(request_ids, half_start + plane % 2 * rows, rows, 0)
        start = first_of_request(request_ids, segments, 2 * grp_size)
        behind = index - start
        first = start - half_start + 2 * half
        first = jnp.maximum(jnp.maximum(first, place - prefix_len + 1), 0)
        turn = rotation(prefix_len + index - start)
        return turn, row_table(behind, first, place), block_bounds(behind, first, place)

    own_turn, *own_rows = table_of(tp_index)
    peer_turn, *peer_rows = table_of(tp_index ^ 1)
    near_keyval = [w_keyval.reshape(width, 2 * kv_cols)]
    far_offsets = owners * (width // grp_size)

    def keyval_of(weights, offsets):
        own = project(normed, weights, offsets, *own_turn, kv_cols)
        other = project(peer, weights, offsets, *peer_turn, kv_cols)
        even = tp_index % 2 == 0
        return jnp.concatenate([jnp.where(even, own, other), jnp.where(even, other, own)], axis=0)

    near = keyval_of(near_keyval, no_offsets)
    far = keyval_of(far_keyval, far_offsets)
    near_suffix = [later(near, 2), later(far, 1), near]
    far_suffix = [later(far, 2), later(near, 1), far]
    page_owner = page_table // pages_dev
    page_rows = ((page_owner ^ grp_index) * pages_dev + page_table % pages_dev) * page_len

    def attend_to(tokens, turn, info, weights, offsets, suffix, column):
        queries = project(tokens, weights, offsets, *turn, w_query.shape[1])
        return attend(
            queries, *info, prefix, page_rows, page_len, suffix, prefix_len, prefix_column=column
        )

    def output_of(tokens, turn, info):
        near_attn = attend_to(tokens, turn, info, [w_query], no_offsets, near_suffix, 0)
        far_attn = attend_to(tokens, turn, info, far_query, far_offsets, far_suffix, 2 * kv_cols)
        return outward(
            [(near_attn, [w_out]), (far_attn, far_out)], owners * (w_out.shape[0] // grp_size)
        )

    received = across(output_of(peer, peer_turn, peer_rows), 1)
    kept = output_of(normed, own_turn, own_rows)
    return (kept.astype(jnp.float32) + received.astype(jnp.float32)).astype(jnp.bfloat16)


def solution(mesh):
    pairs = mesh.shape["tp"] == 4 and mesh.shape["grp"] == 8
    placed = (
        P(("grp", "tp"), None),
        P(),
        P(None, "tp"),
        P(None, None, "tp"),
        P("tp", None),
        P("grp", None, None, "tp"),
        P(),
        P(),
    )
    return jax.shard_map(
        by_pairs if pairs else by_heads,
        mesh=mesh,
        in_specs=placed,
        out_specs=P(("grp", "tp"), None),
        check_vma=False,
    )
```

```python
import functools
import math

import jax
import jax.numpy as jnp
from jax import lax
from jax.experimental import pallas as pl
from jax.experimental.pallas import tpu as pltpu
from jax.sharding import PartitionSpec as P

KVH = 8
HD = 128
SINKS = 4
ROWS = 256
PREFIX_STEP = 512
MASKED = -1e30
EXPONENT = math.log2(math.e) * HD ** (-0.5)
VMEM_LIMIT = 48 * 1024 * 1024


def parameters():
    return pltpu.CompilerParams(vmem_limit_bytes=VMEM_LIMIT)


def whole(*unused):
    return (0, 0)


def gather_columns(order, source, target):
    count = order.shape[0]
    depth = source.shape[1] // count
    for index in range(count):
        start = pl.multiple_of(order[index] * depth, depth)
        target[:, index * depth : (index + 1) * depth] = source[:, pl.ds(start, depth)]


def times_pieces(columns, pieces):
    total = None
    start = 0
    for piece in pieces:
        depth = piece.shape[0]
        term = jnp.dot(
            columns[:, start : start + depth], piece[...], preferred_element_type=jnp.float32
        )
        total = term if total is None else total + term
        start += depth
    return total


def project_kernel(order, *refs, turned, inputs, pieces):
    given = [refs[3 * index : 3 * index + 3] for index in range(inputs)]
    weights = refs[3 * inputs : 3 * inputs + pieces]
    outs = refs[3 * inputs + pieces : 4 * inputs + pieces]
    held = refs[4 * inputs + pieces :]
    if held:

        @pl.when(pl.program_id(0) == 0)
        def fill():
            for (x_ref, *unused), copy in zip(given, held):
                gather_columns(order, x_ref, copy)

    for index, ((x_ref, cos_ref, sin_ref), out_ref) in enumerate(zip(given, outs)):
        total = times_pieces(held[index] if held else x_ref, weights)

        def store(rotated):
            for head in range(out_ref.shape[1] // HD):
                where = slice(head * HD, (head + 1) * HD)
                part = total[:, where]
                if rotated:
                    part = part * cos_ref[...] + pltpu.roll(part, HD // 2, 1) * sin_ref[...]
                out_ref[:, where] = part.astype(out_ref.dtype)

        pl.when(pl.program_id(0) < turned)(lambda: store(True))
        pl.when(pl.program_id(0) >= turned)(lambda: store(False))


def project(inputs, pieces, turned_columns, order=None):
    rows, width = inputs[0][0].shape
    columns = pieces[0].shape[1]
    tile = next(size for size in (512, 256, 128) if turned_columns % size == 0)
    specs, operands = [], []
    for x, cosine, sine in inputs:
        specs += [
            pl.BlockSpec((rows, width), whole),
            pl.BlockSpec((rows, HD), whole),
            pl.BlockSpec((rows, HD), whole),
        ]
        operands += [x, cosine, sine]
    scratch = [] if order is None else [pltpu.VMEM((rows, width), jnp.bfloat16) for unused in inputs]
    outs = pl.pallas_call(
        functools.partial(
            project_kernel,
            turned=turned_columns // tile,
            inputs=len(inputs),
            pieces=len(pieces),
        ),
        out_shape=[jax.ShapeDtypeStruct((rows, columns), jnp.bfloat16) for unused in inputs],
        grid_spec=pltpu.PrefetchScalarGridSpec(
            num_scalar_prefetch=1,
            grid=(columns // tile,),
            in_specs=specs
            + [pl.BlockSpec((piece.shape[0], tile), lambda j, *_: (0, j)) for piece in pieces],
            out_specs=[pl.BlockSpec((rows, tile), lambda j, *_: (0, j)) for unused in inputs],
            scratch_shapes=scratch,
        ),
        compiler_params=parameters(),
        cost_estimate=pl.CostEstimate(
            flops=2 * len(inputs) * rows * width * columns,
            bytes_accessed=2 * (len(inputs) * rows * (width + columns) + width * columns),
            transcendentals=0,
        ),
        name="project",
    )(jnp.zeros((1,), jnp.int32) if order is None else order, *operands, *pieces)
    return outs if len(inputs) > 1 else outs[0]


def stack_heads(source, target):
    rows = source.shape[0]
    for head in range(source.shape[1] // HD):
        target[head * rows : (head + 1) * rows, :] = source[:, head * HD : (head + 1) * HD]


def scores_of(queries, keys, base, size):
    return lax.dot_general(
        queries[...],
        keys[pl.ds(base, size), :],
        (((1,), (1,)), ((), ())),
        preferred_element_type=jnp.float32,
    )


def hide(scores, visible):
    rows = visible.shape[0]
    return jnp.concatenate(
        [
            jnp.where(visible, scores[start : start + rows], MASKED)
            for start in range(0, scores.shape[0], rows)
        ],
        axis=0,
    )


def fold(scores, values, base, size, highest, total):
    after = jnp.broadcast_to(jnp.max(scores, axis=1, keepdims=True), (scores.shape[0], HD))
    if highest is not None:
        after = jnp.maximum(after, highest)
    spread = jnp.concatenate([after] * (size // HD), axis=1)
    weights = jnp.exp2((scores - spread) * EXPONENT)
    term = jnp.dot(
        weights.astype(jnp.bfloat16), values[pl.ds(base, size), :], preferred_element_type=jnp.float32
    )
    if highest is not None:
        factor = jnp.exp2((highest - after) * EXPONENT)
        term = total * jnp.concatenate([factor, factor], axis=1) + term
    return after, term


def prefix_kernel(page_targets, bounds, q_ref, row_ref, *refs, window, page_len, parts):
    cached = refs[: 2 * parts]
    highest, total, queries, keys, values = refs[2 * parts :]
    block = pl.program_id(1)
    prefix_len, rows = keys.shape[0], q_ref.shape[0]
    size = min(PREFIX_STEP, prefix_len)
    steps = prefix_len // size

    @pl.when(block == 0)
    def fill():
        values[:, HD:] = jnp.ones_like(values[:, HD:])
        page = 0
        for part in range(parts):
            key_ref, value_ref = cached[2 * part : 2 * part + 2]
            for start in range(0, key_ref.shape[0], page_len):
                target = pl.ds(pl.multiple_of(page_targets[page], page_len), page_len)
                keys[target, :] = key_ref[start : start + page_len, :]
                values[target, :HD] = value_ref[start : start + page_len, :]
                page += 1

    stack_heads(q_ref, queries)
    behind_min, behind_max = bounds[4 * block], bounds[4 * block + 1]

    def attend_all(masked_steps):
        top = sums = None
        ahead = scores_of(queries, keys, 0, size)
        for step in range(steps):
            scores = ahead
            if step + 1 < steps:
                ahead = scores_of(queries, keys, (step + 1) * size, size)
            if step < masked_steps:
                behind = row_ref[:, 0:1]
                place = step * size + lax.broadcasted_iota(jnp.int32, (rows, size), 1)
                visible = ((place > behind) | (place < SINKS)) & (place <= behind + window)
                scores = hide(scores, visible)
            top, sums = fold(scores, values, step * size, size, top, sums)
        highest[...] = top
        total[...] = sums

    few = min(2, steps)
    plain = (few * size > behind_max) & (prefix_len - 1 <= behind_min + window)
    pl.when(plain)(lambda: attend_all(few))
    pl.when(jnp.logical_not(plain))(lambda: attend_all(steps))


def suffix_kernel(
    targets, bounds, q_ref, row_ref, high_ref, total_ref, *refs, parts, reach
):
    suffix = refs[: 2 * parts]
    out_ref, total, queries, keys, values = refs[2 * parts :]
    block = pl.program_id(1)
    rows = q_ref.shape[0]

    @pl.when(block == 0)
    def fill():
        values[:, HD:] = jnp.ones_like(values[:, HD:])
        for part in range(parts):
            key_ref, value_ref = suffix[2 * part : 2 * part + 2]
            size = key_ref.shape[0]
            target = pl.ds(pl.multiple_of(targets[part], ROWS), size)
            keys[target, :] = key_ref[...]
            values[target, :HD] = value_ref[...]

    stack_heads(q_ref, queries)
    first_min, own_max = bounds[4 * block + 2], bounds[4 * block + 3]
    last = own_max // ROWS
    span = last - jnp.minimum(first_min // ROWS, last)

    def attend_last(count):
        start = pl.multiple_of((last - count + 1) * ROWS, ROWS)
        sizes = [ROWS] * (count % 2) + [2 * ROWS] * (count // 2)
        bases = [pl.multiple_of(start + sum(sizes[:step]), ROWS) for step in range(len(sizes))]
        top, sums = high_ref[...], total_ref[...]
        ahead = scores_of(queries, keys, bases[0], sizes[0])
        for step, (base, size) in enumerate(zip(bases, sizes)):
            scores = ahead
            if step + 1 < len(sizes):
                ahead = scores_of(queries, keys, bases[step + 1], sizes[step + 1])
            place = base + lax.broadcasted_iota(jnp.int32, (rows, size), 1)
            visible = (place >= row_ref[:, 1:2]) & (place <= row_ref[:, 2:3])
            top, sums = fold(hide(scores, visible), values, base, size, top, sums)
        total[...] = sums

    for count in range(1, reach // ROWS + 2):
        pl.when(span == count - 1)(functools.partial(attend_last, count))
    for head in range(q_ref.shape[1] // HD):
        mine = slice(head * rows, (head + 1) * rows)
        out_ref[:, head * HD : (head + 1) * HD] = (total[mine, :HD] / total[mine, HD:]).astype(
            out_ref.dtype
        )


def key_and_value(rows, block, column, kv_heads):
    at = column // HD
    return [
        pl.BlockSpec((rows, HD), lambda h, i, *_: (block, at + h)),
        pl.BlockSpec((rows, HD), lambda h, i, *_: (block, at + kv_heads + h)),
    ]


def block_of(columns, skip=0):
    return pl.BlockSpec((ROWS, columns), lambda h, i, *_: (skip + i, h))


def state_specs(rows, share, skip=0):
    stacked = ROWS * share // HD

    def place(h, i, *unused):
        return (h * (rows // ROWS) + skip + i, 0)

    return [pl.BlockSpec((stacked, HD), place), pl.BlockSpec((stacked, 2 * HD), place)]


def attend_prefix(queries, info, parts, page_targets, page_len, window, kv_heads):
    row_info, bounds = info
    rows, columns = queries.shape
    share = columns // kv_heads
    count = sum(array.shape[0] for array, unused in parts)
    specs, operands = [], []
    for array, column in parts:
        specs += key_and_value(array.shape[0], 0, column, kv_heads)
        operands += [array, array]
    return pl.pallas_call(
        functools.partial(prefix_kernel, window=window, page_len=page_len, parts=len(parts)),
        out_shape=[
            jax.ShapeDtypeStruct((rows * columns // HD, HD), jnp.float32),
            jax.ShapeDtypeStruct((rows * columns // HD, 2 * HD), jnp.float32),
        ],
        grid_spec=pltpu.PrefetchScalarGridSpec(
            num_scalar_prefetch=2,
            grid=(kv_heads, rows // ROWS),
            in_specs=[block_of(share), pl.BlockSpec((ROWS, HD), lambda h, i, *_: (i, 0))] + specs,
            out_specs=state_specs(rows, share),
            scratch_shapes=[
                pltpu.VMEM((ROWS * share // HD, HD), jnp.bfloat16),
                pltpu.VMEM((count, HD), jnp.bfloat16),
                pltpu.VMEM((count, 2 * HD), jnp.bfloat16),
            ],
        ),
        compiler_params=parameters(),
        cost_estimate=pl.CostEstimate(
            flops=12 * rows * columns * count,
            bytes_accessed=14 * queries.size + 4 * kv_heads * HD * count,
            transcendentals=rows * columns // HD * count,
        ),
        name="attend_prefix",
    )(page_targets, bounds, queries, row_info, *operands)


def attend_suffix(queries, info, state, parts, targets, kv_heads, reach, blocks=None):
    row_info, bounds = info
    rows, columns = queries.shape
    share = columns // kv_heads
    skip, number = (0, rows // ROWS) if blocks is None else blocks
    bounds = bounds[4 * skip : 4 * (skip + number)]
    count = sum(size for unused, size, *unused in parts)
    specs, operands = [], []
    for array, size, block, column in parts:
        specs += key_and_value(size, block, column, kv_heads)
        operands += [array, array]
    return pl.pallas_call(
        functools.partial(suffix_kernel, parts=len(parts), reach=reach),
        out_shape=jax.ShapeDtypeStruct((number * ROWS, columns), jnp.bfloat16),
        grid_spec=pltpu.PrefetchScalarGridSpec(
            num_scalar_prefetch=2,
            grid=(kv_heads, number),
            in_specs=[
                block_of(share, skip),
                pl.BlockSpec((ROWS, HD), lambda h, i, *_: (skip + i, 0)),
            ]
            + state_specs(rows, share, skip)
            + specs,
            out_specs=block_of(share),
            scratch_shapes=[
                pltpu.VMEM((ROWS * share // HD, 2 * HD), jnp.float32),
                pltpu.VMEM((ROWS * share // HD, HD), jnp.bfloat16),
                pltpu.VMEM((count, HD), jnp.bfloat16),
                pltpu.VMEM((count, 2 * HD), jnp.bfloat16),
            ],
        ),
        compiler_params=parameters(),
        cost_estimate=pl.CostEstimate(
            flops=6 * number * ROWS * columns * count,
            bytes_accessed=16 * queries.size + 4 * kv_heads * HD * count,
            transcendentals=number * ROWS * columns // HD * count // 2,
        ),
        name="attend_suffix",
    )(targets, bounds, queries, row_info, *state, *operands)


def outward_kernel(order, *refs, parts):
    count = len(parts)
    attns, weights = refs[:count], refs[count : count + sum(parts)]
    out_ref, *held = refs[count + sum(parts) :]
    if held:

        @pl.when(pl.program_id(0) == 0)
        def fill():
            gather_columns(order, attns[-1], held[0])

    total = None
    at = 0
    for index, pieces in enumerate(parts):
        columns = held[0] if held and index == count - 1 else attns[index]
        term = times_pieces(columns, weights[at : at + pieces])
        total = term if total is None else total + term
        at += pieces
    out_ref[...] = total.astype(out_ref.dtype)


def outward(pairs, order=None, window=None):
    rows = pairs[0][0].shape[0]
    first, columns = (0, pairs[0][1][0].shape[1]) if window is None else window
    tile = min(1024, columns)
    attns = [attn for attn, unused in pairs]
    pieces = [piece for unused, stack in pairs for piece in stack]
    skips = [(piece.shape[1] > columns) * (first // tile) for piece in pieces]
    depth = sum(piece.shape[0] for piece in pieces)
    scratch = [] if order is None else [pltpu.VMEM(attns[-1].shape, jnp.bfloat16)]

    def tile_of(piece, skip):
        return pl.BlockSpec((piece.shape[0], tile), lambda j, *_: (0, skip + j))

    return pl.pallas_call(
        functools.partial(outward_kernel, parts=tuple(len(stack) for unused, stack in pairs)),
        out_shape=jax.ShapeDtypeStruct((rows, columns), jnp.bfloat16),
        grid_spec=pltpu.PrefetchScalarGridSpec(
            num_scalar_prefetch=1,
            grid=(columns // tile,),
            in_specs=[pl.BlockSpec(attn.shape, whole) for attn in attns]
            + [tile_of(piece, skip) for piece, skip in zip(pieces, skips)],
            out_specs=pl.BlockSpec((rows, tile), lambda j, *_: (0, j)),
            scratch_shapes=scratch,
        ),
        compiler_params=parameters(),
        cost_estimate=pl.CostEstimate(
            flops=2 * rows * columns * depth,
            bytes_accessed=2 * (columns * (rows + depth) + rows * depth),
            transcendentals=0,
        ),
        name="outward",
    )(jnp.zeros((1,), jnp.int32) if order is None else order, *attns, *pieces)


def rotation(positions):
    half = HD // 2
    freqs = 500000.0 ** (-jnp.arange(half, dtype=jnp.float32) * 2.0 / HD)
    angles = positions.astype(jnp.float32)[:, None] * freqs[None, :]
    cosine, sine = jnp.cos(angles), jnp.sin(angles)
    return jnp.concatenate([cosine, cosine], axis=1), jnp.concatenate([-sine, sine], axis=1)


def table_and_bounds(behind, first, place):
    rows = behind.shape[0]
    table = jnp.stack([behind, first, place], axis=1).astype(jnp.int32)
    table = jnp.concatenate([table, jnp.zeros((rows, HD - 3), jnp.int32)], axis=1)

    def blocks(array):
        return array.reshape(-1, ROWS)

    bounds = jnp.stack(
        [
            blocks(behind).min(axis=1),
            blocks(behind).max(axis=1),
            blocks(first).min(axis=1),
            blocks(place).max(axis=1),
        ],
        axis=1,
    )
    return table, bounds.reshape(-1).astype(jnp.int32)


def normalize(x_rows, norm_gain):
    wide = x_rows.astype(jnp.float32)
    variance = jnp.mean(wide * wide, axis=-1, keepdims=True) + 1e-05
    return (wide * lax.rsqrt(variance) * norm_gain).astype(jnp.bfloat16)


def first_of_request(request_ids, wanted, count):
    labels = jnp.arange(count, dtype=jnp.int32)
    counts = jnp.sum((request_ids[:, None] == labels[None, :]).astype(jnp.int32), axis=0)
    starts = jnp.cumsum(counts) - counts
    match = wanted[:, None] == labels[None, :]
    return jnp.sum(jnp.where(match, starts[None, :], 0), axis=1)


def logical_pages(page_table, physical):
    labels = jnp.arange(page_table.shape[0], dtype=jnp.int32)
    match = page_table[None, :] == physical[:, None]
    return jnp.sum(jnp.where(match, labels[None, :], 0), axis=1)


def join_pair(lower, mine, peer):
    return jnp.where(
        lower, jnp.concatenate([mine, peer], axis=2), jnp.concatenate([peer, mine], axis=2)
    )


def swapped(block, axis, apart):
    route = [(i, i ^ 1 << apart) for i in range(lax.axis_size(axis))]
    return lax.ppermute(block, axis, route)


def shifted(block, axis, distance):
    route = [(i, i + distance) for i in range(lax.axis_size(axis) - distance)]
    return lax.ppermute(block, axis, route)


def by_heads(x_rows, norm_gain, w_query, w_keyval, w_out, prefix_cache, page_table, request_ids):
    tp_size = lax.axis_size("tp")
    grp_size = lax.axis_size("grp")
    tp_index = lax.axis_index("tp")
    grp_index = lax.axis_index("grp")
    tok_group = x_rows.shape[0] * tp_size
    kv_cols = w_keyval.shape[2]
    kv_need = max(HD, HD * KVH // tp_size)
    kv_heads = kv_need // HD
    pages_dev, page_len = prefix_cache.shape[:2]
    prefix_len = pages_dev * grp_size * page_len
    pair_bits = (kv_need // kv_cols).bit_length() - 1

    normed = normalize(x_rows, norm_gain)
    tokens = lax.all_gather(normed, "tp", axis=0, tiled=True)
    group_start = grp_index * tok_group
    token_index = group_start + jnp.arange(tok_group, dtype=jnp.int32)
    own_seg = lax.dynamic_slice_in_dim(request_ids, group_start, tok_group, 0)
    own_first = first_of_request(request_ids, own_seg, 2 * grp_size)
    own_pos = prefix_len + token_index - own_first
    cosine, sine = rotation(own_pos)
    given = [(tokens, cosine, sine)]
    queries = project(given, [w_query], w_query.shape[1])
    kv_weight = w_keyval.reshape(w_keyval.shape[0], 2 * kv_cols)
    cache = prefix_cache.reshape(pages_dev * page_len, 2, kv_cols)
    if pair_bits == 0:
        own = project(given, [kv_weight], kv_cols)
    else:
        keyval = jnp.dot(tokens, kv_weight, preferred_element_type=jnp.float32)
        keyval = keyval.astype(jnp.bfloat16).reshape(tok_group, 2, kv_cols)
        for bit_num in range(pair_bits):
            lower = tp_index >> bit_num & 1 == 0
            keyval = join_pair(lower, keyval, swapped(keyval, "tp", bit_num))
            cache = join_pair(lower, cache, swapped(cache, "tp", bit_num))
        keys = keyval[:, 0].astype(jnp.float32).reshape(tok_group, -1, HD)
        keys = keys * cosine[:, None] + jnp.roll(keys, HD // 2, axis=2) * sine[:, None]
        keys = keys.reshape(tok_group, kv_need).astype(jnp.bfloat16)
        own = jnp.concatenate([keys, keyval[:, 1]], axis=1)
    before = shifted(own, "grp", 1)
    cache = cache.reshape(pages_dev * page_len, 2 * kv_need)
    prefix = lax.all_gather(cache, "grp", axis=0, tiled=True)
    place = tok_group + jnp.arange(tok_group, dtype=jnp.int32)
    first = own_first - group_start + tok_group
    first = jnp.maximum(jnp.maximum(first, place - prefix_len + 1), 0)
    info = table_and_bounds(own_pos - prefix_len, first, place)
    physical = jnp.arange(page_table.shape[0], dtype=jnp.int32)
    targets = logical_pages(page_table, physical) * page_len
    state = attend_prefix(
        queries, info, [(prefix, 0)], targets, page_len, prefix_len, kv_heads
    )
    attn = attend_suffix(
        queries,
        info,
        state,
        [(before, tok_group, 0, 0), (own, tok_group, 0, 0)],
        jnp.array([0, tok_group], jnp.int32),
        kv_heads,
        tok_group,
    )
    return lax.psum_scatter(
        outward([(attn, [w_out])]), "tp", scatter_dimension=0, tiled=True
    )


def by_pairs(x_rows, norm_gain, w_query, w_keyval, w_out, prefix_cache, page_table, request_ids):
    grp_size = lax.axis_size("grp")
    tp_size = lax.axis_size("tp")
    grp_index = lax.axis_index("grp")
    tp_index = lax.axis_index("tp")
    rows, width = x_rows.shape
    kv_cols = w_keyval.shape[2]
    kv_heads = kv_cols // HD
    query_cols = w_query.shape[1]
    pages_dev, page_len = prefix_cache.shape[:2]
    prefix_len = pages_dev * grp_size * page_len
    half = 2 * rows
    sync = lax.optimization_barrier

    def across(block, distance):
        return lax.ppermute(block, "tp", [(i, i ^ distance) for i in range(tp_size)])

    def within(block, even, odd):
        route = [(i, i ^ (odd if i % 2 else even)) for i in range(grp_size)]
        return lax.ppermute(block, "grp", route)

    def swap_first(block):
        return within(block, 2, 4)

    def swap_second(pair):
        return within(pair, 4, 2)

    def swap_core(four):
        return within(four, 1, 1)

    def under(*blocks):
        return jnp.concatenate(blocks, axis=0)

    def share_of(weight):
        part = weight.shape[0] // grp_size
        return lax.dynamic_slice_in_dim(weight, grp_index * part, part, 0)

    def later(block, by):
        route = []
        for place in range(2 * grp_size - by):
            target = place + by
            for side in range(2):
                source_id = place // 2 * tp_size + place % 2 * 2 + side
                target_id = target // 2 * tp_size + target % 2 * 2 + side
                route.append((source_id, target_id))
        return lax.ppermute(block, ("grp", "tp"), route)

    odd = grp_index % 2
    first_hop, second_hop = 2 + 2 * odd, 4 - 2 * odd
    hops = [0, first_hop, second_hop, 6, 1, 1 ^ second_hop, 1 ^ first_hop, 7]
    order = grp_index ^ jnp.stack([jnp.int32(hop) for hop in hops])
    half_order = jnp.concatenate([2 * order, 2 * order + 1])
    half_start = grp_index * rows * tp_size + tp_index // 2 * half

    def rows_of(plane):
        place = 2 * half + plane % 2 * rows + jnp.arange(rows, dtype=jnp.int32)
        index = half_start - 2 * half + place
        segments = lax.dynamic_slice_in_dim(request_ids, half_start + plane % 2 * rows, rows, 0)
        return index, place, segments

    index, place, segments = [
        under(*pair) for pair in zip(rows_of(tp_index), rows_of(tp_index ^ 1))
    ]

    normed = normalize(x_rows, norm_gain)
    keyval_share = share_of(w_keyval).reshape(width // grp_size, 2 * kv_cols)
    query_share = share_of(w_query)
    part = query_share.shape[0] // 2
    normed, keyval_share, query_a, query_b = sync(
        (normed, keyval_share, query_share[:part], query_share[part:])
    )
    middle = rows // 2
    far_keyval = across(keyval_share, 2)
    far_a = across(query_a, 2)
    peer_a = across(normed[:middle], 1)
    near_cache = prefix_cache.reshape(pages_dev * page_len, 2 * kv_cols)
    cache_near = lax.all_gather(near_cache, "grp", axis=0, tiled=True)
    start = first_of_request(request_ids, segments, 2 * grp_size)
    first = start - half_start + 2 * half
    first = jnp.maximum(jnp.maximum(first, place - prefix_len + 1), 0)
    cosine, sine = rotation(prefix_len + index - start)
    table, bounds = table_and_bounds(index - start, first, place)
    near_keyval = w_keyval.reshape(width, 2 * kv_cols)
    physical = jnp.arange(page_table.shape[0], dtype=jnp.int32)
    page_targets = logical_pages(page_table, physical) * page_len
    low = tp_index % 2 * rows
    targets = jnp.stack(
        [base + side for base in (0, half, 2 * half) for side in (low, rows - low)]
    ).astype(jnp.int32)
    (
        far_keyval, far_a, peer_a, query_b, near_cache, near_keyval, cosine, sine, table, bounds, normed
    ) = sync(
        (far_keyval, far_a, peer_a, query_b, near_cache, near_keyval, cosine, sine, table, bounds, normed)
    )

    keyval_pair = under(far_keyval, swap_first(far_keyval))
    pair_a = under(far_a, swap_first(far_a))
    far_b = across(query_b, 2)
    far_cache = across(near_cache, 2)
    peer_b = across(normed[middle:], 1)
    out_share = share_of(w_out)
    cut = w_out.shape[1] // 4 * 3
    keyval_pair, pair_a, far_b, far_cache, peer_b, normed, out_a, out_b = sync(
        (keyval_pair, pair_a, far_b, far_cache, peer_b, normed, out_share[:, :cut], out_share[:, cut:])
    )

    keyval_four = under(keyval_pair, swap_second(keyval_pair))
    four_a = under(pair_a, swap_second(pair_a))
    pair_b = under(far_b, swap_first(far_b))
    out_a = across(out_a, 2)
    tokens = under(normed, peer_a, peer_b)
    given = [(tokens, cosine, sine)]
    near_kv = project(given, [near_keyval], kv_cols)
    near_q = project(given, [w_query], query_cols)
    keyval_four, four_a, pair_b, tokens, out_a, out_b, near_kv, near_q, far_cache = sync(
        (keyval_four, four_a, pair_b, tokens, out_a, out_b, near_kv, near_q, far_cache)
    )

    cache_far = lax.all_gather(far_cache, "grp", axis=0, tiled=True)
    keyval_others = swap_core(keyval_four)
    others_a = swap_core(four_a)
    four_b = under(pair_b, swap_second(pair_b))
    near_two, near_one = later(near_kv, 2), later(near_kv, 1)
    info = (table, bounds)

    def prefix_of(queries, cache):
        return attend_prefix(
            queries, info, [(cache, 0)], page_targets, page_len, prefix_len, kv_heads
        )

    near_state = prefix_of(near_q, cache_near)
    keyval_others, others_a, four_b, near_two, near_one, near_state, tokens, out_a, out_b = sync(
        (keyval_others, others_a, four_b, near_two, near_one, near_state, tokens, out_a, out_b)
    )

    given = [(tokens, cosine, sine)]
    others_b = swap_core(four_b)
    out_pair_a = under(out_a, swap_first(out_a))
    out_b = across(out_b, 2)
    far_kv = project(given, [keyval_four, keyval_others], kv_cols, order)
    others_b, out_pair_a, out_b, far_kv, tokens = sync(
        (others_b, out_pair_a, out_b, far_kv, tokens)
    )

    far_two, far_one = later(far_kv, 2), later(far_kv, 1)
    out_four_a = under(out_pair_a, swap_second(out_pair_a))
    out_pair_b = under(out_b, swap_first(out_b))
    given = [(tokens, cosine, sine)]
    far_q = project(given, [four_a, others_a, four_b, others_b], query_cols, half_order)
    far_state = prefix_of(far_q, cache_far)
    far_two, far_one, out_four_a, out_pair_b, far_state, far_q = sync(
        (far_two, far_one, out_four_a, out_pair_b, far_state, far_q)
    )

    def suffix_of(queries, state, two, one, own, block):
        parts = [(array, rows, index, 0) for array in (two, one, own) for index in range(2)]
        return attend_suffix(
            queries, info, state, parts, targets, kv_heads, tp_size * rows, (block, 1)
        )

    out_others_a = swap_core(out_four_a)
    out_four_b = under(out_pair_b, swap_second(out_pair_b))
    peer_near = suffix_of(near_q, near_state, near_two, far_one, near_kv, 1)
    peer_far = suffix_of(far_q, far_state, far_two, near_one, far_kv, 1)
    out_others_a, out_four_b, peer_near, peer_far = sync(
        (out_others_a, out_four_b, peer_near, peer_far)
    )

    def output_of(near_attn, far_attn, weights, at, columns):
        return outward([(near_attn, [w_out]), (far_attn, weights)], order, (at, columns))

    rest = w_out.shape[1] - cut
    out_others_b = swap_core(out_four_b)
    sent_a = output_of(peer_near, peer_far, [out_four_a, out_others_a], 0, cut)
    out_others_b, sent_a, peer_near = sync((out_others_b, sent_a, peer_near))

    received_a = across(sent_a, 1)
    sent_b = output_of(peer_near, peer_far, [out_four_b, out_others_b], cut, rest)
    received_b = across(sent_b, 1)
    own_near = suffix_of(sync((near_q, sent_b))[0], near_state, near_two, far_one, near_kv, 0)
    own_far = suffix_of(sync((far_q, own_near))[0], far_state, far_two, near_one, far_kv, 0)
    kept_a = output_of(own_near, own_far, [out_four_a, out_others_a], 0, cut)
    kept_b = output_of(own_near, own_far, [out_four_b, out_others_b], cut, rest)
    sums = [
        (mine.astype(jnp.float32) + theirs.astype(jnp.float32)).astype(jnp.bfloat16)
        for mine, theirs in ((kept_a, received_a), (kept_b, received_b))
    ]
    return jnp.concatenate(sums, axis=1)


def solution(mesh):
    pairs = mesh.shape["tp"] == 4 and mesh.shape["grp"] == 8
    placed = (
        P(("grp", "tp"), None),
        P(),
        P(None, "tp"),
        P(None, None, "tp"),
        P("tp", None),
        P("grp", None, None, "tp"),
        P(),
        P(),
    )
    return jax.shard_map(
        by_pairs if pairs else by_heads,
        mesh=mesh,
        in_specs=placed,
        out_specs=P(("grp", "tp"), None),
        check_vma=False,
    )
```

```python
import functools
import math

import jax
import jax.numpy as jnp
from jax import lax
from jax.experimental import pallas as pl
from jax.experimental.pallas import tpu as pltpu
from jax.sharding import PartitionSpec as P

KVH = 8
HD = 128
SINKS = 4
ROWS = 256
PREFIX_STEP = 512
MASKED = -1e30
EXPONENT = math.log2(math.e) * HD ** (-0.5)
VMEM_LIMIT = 48 * 1024 * 1024


def parameters():
    return pltpu.CompilerParams(vmem_limit_bytes=VMEM_LIMIT)


def whole(*unused):
    return (0, 0)


def gather_columns(starts, depths, source, target):
    at = 0
    for index, depth in enumerate(depths):
        start = pl.multiple_of(starts[index] * HD, HD)
        target[:, at : at + depth] = source[:, pl.ds(start, depth)]
        at += depth


def times_pieces(columns, pieces):
    total = None
    start = 0
    for piece in pieces:
        depth = piece.shape[0]
        term = jnp.dot(
            columns[:, start : start + depth], piece[...], preferred_element_type=jnp.float32
        )
        total = term if total is None else total + term
        start += depth
    return total


def project_kernel(starts, *refs, turned, inputs, pieces, depths):
    given = [refs[3 * index : 3 * index + 3] for index in range(inputs)]
    weights = refs[3 * inputs : 3 * inputs + pieces]
    outs = refs[3 * inputs + pieces : 4 * inputs + pieces]
    held = refs[4 * inputs + pieces :]
    if held:

        @pl.when(pl.program_id(0) == 0)
        def fill():
            for (x_ref, *unused), copy in zip(given, held):
                gather_columns(starts, depths, x_ref, copy)

    for index, ((x_ref, cos_ref, sin_ref), out_ref) in enumerate(zip(given, outs)):
        total = times_pieces(held[index] if held else x_ref, weights)

        def store(rotated):
            for head in range(out_ref.shape[1] // HD):
                where = slice(head * HD, (head + 1) * HD)
                part = total[:, where]
                if rotated:
                    part = part * cos_ref[...] + pltpu.roll(part, HD // 2, 1) * sin_ref[...]
                out_ref[:, where] = part.astype(out_ref.dtype)

        pl.when(pl.program_id(0) < turned)(lambda: store(True))
        pl.when(pl.program_id(0) >= turned)(lambda: store(False))


def project(inputs, pieces, turned_columns, starts=None, depths=(), block=None):
    rows, width = inputs[0][0].shape
    rows, at = (rows, 0) if block is None else block
    columns = pieces[0].shape[1]
    tile = next(size for size in (512, 256, 128) if turned_columns % size == 0)
    specs, operands = [], []
    for x, cosine, sine in inputs:
        specs += [
            pl.BlockSpec((rows, width), lambda *unused: (at, 0)),
            pl.BlockSpec((rows, HD), lambda *unused: (at, 0)),
            pl.BlockSpec((rows, HD), lambda *unused: (at, 0)),
        ]
        operands += [x, cosine, sine]
    scratch = [] if starts is None else [pltpu.VMEM((rows, width), jnp.bfloat16) for unused in inputs]
    outs = pl.pallas_call(
        functools.partial(
            project_kernel,
            turned=turned_columns // tile,
            inputs=len(inputs),
            pieces=len(pieces),
            depths=depths,
        ),
        out_shape=[jax.ShapeDtypeStruct((rows, columns), jnp.bfloat16) for unused in inputs],
        grid_spec=pltpu.PrefetchScalarGridSpec(
            num_scalar_prefetch=1,
            grid=(columns // tile,),
            in_specs=specs
            + [pl.BlockSpec((piece.shape[0], tile), lambda j, *_: (0, j)) for piece in pieces],
            out_specs=[pl.BlockSpec((rows, tile), lambda j, *_: (0, j)) for unused in inputs],
            scratch_shapes=scratch,
        ),
        compiler_params=parameters(),
        cost_estimate=pl.CostEstimate(
            flops=2 * len(inputs) * rows * width * columns,
            bytes_accessed=2 * (len(inputs) * rows * (width + columns) + width * columns),
            transcendentals=0,
        ),
        name="project",
    )(jnp.zeros((1,), jnp.int32) if starts is None else starts, *operands, *pieces)
    return outs if len(inputs) > 1 else outs[0]


def stack_heads(source, target):
    rows = source.shape[0]
    for head in range(source.shape[1] // HD):
        target[head * rows : (head + 1) * rows, :] = source[:, head * HD : (head + 1) * HD]


def scores_of(queries, keys, base, size):
    return lax.dot_general(
        queries[...],
        keys[pl.ds(base, size), :],
        (((1,), (1,)), ((), ())),
        preferred_element_type=jnp.float32,
    )


def hide(scores, visible):
    rows = visible.shape[0]
    return jnp.concatenate(
        [
            jnp.where(visible, scores[start : start + rows], MASKED)
            for start in range(0, scores.shape[0], rows)
        ],
        axis=0,
    )


def fold(scores, values, base, size, highest, total):
    after = jnp.broadcast_to(jnp.max(scores, axis=1, keepdims=True), (scores.shape[0], HD))
    if highest is not None:
        after = jnp.maximum(after, highest)
    spread = jnp.concatenate([after] * (size // HD), axis=1)
    weights = jnp.exp2((scores - spread) * EXPONENT)
    term = jnp.dot(
        weights.astype(jnp.bfloat16), values[pl.ds(base, size), :], preferred_element_type=jnp.float32
    )
    if highest is not None:
        factor = jnp.exp2((highest - after) * EXPONENT)
        term = total * jnp.concatenate([factor, factor], axis=1) + term
    return after, term


def prefix_kernel(page_targets, bounds, q_ref, row_ref, *refs, window, page_len, parts):
    cached = refs[: 2 * parts]
    highest, total, queries, keys, values = refs[2 * parts :]
    block = pl.program_id(1)
    prefix_len, rows = keys.shape[0], q_ref.shape[0]
    size = min(PREFIX_STEP, prefix_len)
    steps = prefix_len // size

    @pl.when(block == 0)
    def fill():
        values[:, HD:] = jnp.ones_like(values[:, HD:])
        page = 0
        for part in range(parts):
            key_ref, value_ref = cached[2 * part : 2 * part + 2]
            for start in range(0, key_ref.shape[0], page_len):
                target = pl.ds(pl.multiple_of(page_targets[page], page_len), page_len)
                keys[target, :] = key_ref[start : start + page_len, :]
                values[target, :HD] = value_ref[start : start + page_len, :]
                page += 1

    stack_heads(q_ref, queries)
    behind_min, behind_max = bounds[4 * block], bounds[4 * block + 1]

    def attend_all(masked_steps):
        top = sums = None
        ahead = scores_of(queries, keys, 0, size)
        for step in range(steps):
            scores = ahead
            if step + 1 < steps:
                ahead = scores_of(queries, keys, (step + 1) * size, size)
            if step < masked_steps:
                behind = row_ref[:, 0:1]
                place = step * size + lax.broadcasted_iota(jnp.int32, (rows, size), 1)
                visible = ((place > behind) | (place < SINKS)) & (place <= behind + window)
                scores = hide(scores, visible)
            top, sums = fold(scores, values, step * size, size, top, sums)
        highest[...] = top
        total[...] = sums

    few = min(2, steps)
    plain = (few * size > behind_max) & (prefix_len - 1 <= behind_min + window)
    pl.when(plain)(lambda: attend_all(few))
    pl.when(jnp.logical_not(plain))(lambda: attend_all(steps))


def suffix_kernel(targets, bounds, row_ref, *refs, parts, reach, groups, kv_heads):
    each = 3 + 2 * parts
    out_ref, total, queries, keys, values = refs[groups * each :]
    block = pl.program_id(1)
    rows = row_ref.shape[0]
    first_min, own_max = bounds[4 * block + 2], bounds[4 * block + 3]
    last = own_max // ROWS
    span = last - jnp.minimum(first_min // ROWS, last)

    def prepare(group):
        q_ref, high_ref, total_ref, *suffix = refs[group * each : (group + 1) * each]

        @pl.when(block == 0)
        def fill():
            values[:, HD:] = jnp.ones_like(values[:, HD:])
            for part in range(parts):
                key_ref, value_ref = suffix[2 * part : 2 * part + 2]
                size = key_ref.shape[0]
                target = pl.ds(pl.multiple_of(targets[part], ROWS), size)
                keys[target, :] = key_ref[...]
                values[target, :HD] = value_ref[...]

        stack_heads(q_ref, queries)

        def attend_last(count):
            start = pl.multiple_of((last - count + 1) * ROWS, ROWS)
            sizes = [ROWS] * (count % 2) + [2 * ROWS] * (count // 2)
            bases = [pl.multiple_of(start + sum(sizes[:step]), ROWS) for step in range(len(sizes))]
            top, sums = high_ref[...], total_ref[...]
            ahead = scores_of(queries, keys, bases[0], sizes[0])
            for step, (base, size) in enumerate(zip(bases, sizes)):
                scores = ahead
                if step + 1 < len(sizes):
                    ahead = scores_of(queries, keys, bases[step + 1], sizes[step + 1])
                place = base + lax.broadcasted_iota(jnp.int32, (rows, size), 1)
                visible = (place >= row_ref[:, 1:2]) & (place <= row_ref[:, 2:3])
                top, sums = fold(hide(scores, visible), values, base, size, top, sums)
            total[...] = sums

        for count in range(1, reach // ROWS + 2):
            pl.when(span == count - 1)(functools.partial(attend_last, count))

    for group in range(groups):
        pl.when(pl.program_id(0) // kv_heads == group)(functools.partial(prepare, group))
    for head in range(out_ref.shape[1] // HD):
        mine = slice(head * rows, (head + 1) * rows)
        out_ref[:, head * HD : (head + 1) * HD] = (total[mine, :HD] / total[mine, HD:]).astype(
            out_ref.dtype
        )


def key_and_value(rows, block, column, kv_heads):
    at = column // HD
    return [
        pl.BlockSpec((rows, HD), lambda h, i, *_: (block, at + h)),
        pl.BlockSpec((rows, HD), lambda h, i, *_: (block, at + kv_heads + h)),
    ]


def state_specs(rows, share):
    stacked = ROWS * share // HD

    def place(h, i, *unused):
        return (h * (rows // ROWS) + i, 0)

    return [pl.BlockSpec((stacked, HD), place), pl.BlockSpec((stacked, 2 * HD), place)]


def attend_prefix(queries, info, parts, page_targets, page_len, window, kv_heads, at=0):
    row_info, bounds = info
    rows, columns = row_info.shape[0], queries.shape[1]
    share = columns // kv_heads
    count = sum(array.shape[0] for array, unused in parts)
    specs, operands = [], []
    for array, column in parts:
        specs += key_and_value(array.shape[0], 0, column, kv_heads)
        operands += [array, array]
    return pl.pallas_call(
        functools.partial(prefix_kernel, window=window, page_len=page_len, parts=len(parts)),
        out_shape=[
            jax.ShapeDtypeStruct((rows * columns // HD, HD), jnp.float32),
            jax.ShapeDtypeStruct((rows * columns // HD, 2 * HD), jnp.float32),
        ],
        grid_spec=pltpu.PrefetchScalarGridSpec(
            num_scalar_prefetch=2,
            grid=(kv_heads, rows // ROWS),
            in_specs=[
                pl.BlockSpec((ROWS, share), lambda h, i, *_: (at + i, h)),
                pl.BlockSpec((ROWS, HD), lambda h, i, *_: (i, 0)),
            ]
            + specs,
            out_specs=state_specs(rows, share),
            scratch_shapes=[
                pltpu.VMEM((ROWS * share // HD, HD), jnp.bfloat16),
                pltpu.VMEM((count, HD), jnp.bfloat16),
                pltpu.VMEM((count, 2 * HD), jnp.bfloat16),
            ],
        ),
        compiler_params=parameters(),
        cost_estimate=pl.CostEstimate(
            flops=12 * rows * columns * count,
            bytes_accessed=14 * rows * columns + 4 * kv_heads * HD * count,
            transcendentals=rows * columns // HD * count,
        ),
        name="attend_prefix",
    )(page_targets, bounds, queries, row_info, *operands)


def attend_suffix(groups, info, targets, kv_heads, reach):
    row_info, bounds = info
    number, columns = row_info.shape[0] // ROWS, groups[0][0].shape[1]
    share = columns // kv_heads
    stacked = ROWS * share // HD
    count = sum(size for array, size, block in groups[0][4])
    specs = [pl.BlockSpec((ROWS, HD), lambda h, i, *_: (i, 0))]
    operands = [row_info]
    for group, (queries, state, skip, state_skip, parts) in enumerate(groups):
        state_blocks = state[0].shape[0] // (stacked * kv_heads)

        def head_of(h, group=group):
            return jnp.clip(h - group * kv_heads, 0, kv_heads - 1)

        def query_at(h, i, *unused, head_of=head_of, skip=skip):
            return (skip + i, head_of(h))

        def state_at(h, i, *unused, head_of=head_of, blocks=state_blocks, skip=state_skip):
            return (head_of(h) * blocks + skip + i, 0)

        specs += [
            pl.BlockSpec((ROWS, share), query_at),
            pl.BlockSpec((stacked, HD), state_at),
            pl.BlockSpec((stacked, 2 * HD), state_at),
        ]
        operands += [queries, *state]
        for array, size, block in parts:
            for at in (0, kv_heads):

                def part_at(h, i, *unused, head_of=head_of, block=block, at=at):
                    return (block, at + head_of(h))

                specs.append(pl.BlockSpec((size, HD), part_at))
                operands.append(array)
    return pl.pallas_call(
        functools.partial(
            suffix_kernel,
            parts=len(groups[0][4]),
            reach=reach,
            groups=len(groups),
            kv_heads=kv_heads,
        ),
        out_shape=jax.ShapeDtypeStruct((number * ROWS, len(groups) * columns), jnp.bfloat16),
        grid_spec=pltpu.PrefetchScalarGridSpec(
            num_scalar_prefetch=2,
            grid=(len(groups) * kv_heads, number),
            in_specs=specs,
            out_specs=pl.BlockSpec((ROWS, share), lambda h, i, *_: (i, h)),
            scratch_shapes=[
                pltpu.VMEM((stacked, 2 * HD), jnp.float32),
                pltpu.VMEM((stacked, HD), jnp.bfloat16),
                pltpu.VMEM((count, HD), jnp.bfloat16),
                pltpu.VMEM((count, 2 * HD), jnp.bfloat16),
            ],
        ),
        compiler_params=parameters(),
        cost_estimate=pl.CostEstimate(
            flops=6 * number * ROWS * columns * count * len(groups),
            bytes_accessed=16 * number * ROWS * columns * len(groups),
            transcendentals=number * ROWS * columns // HD * count // 2 * len(groups),
        ),
        name="attend_suffix",
    )(targets, bounds, *operands)


def outward_kernel(starts, *refs, parts, depths):
    count = len(parts)
    attns, weights = refs[:count], refs[count : count + sum(parts)]
    out_ref, *held = refs[count + sum(parts) :]
    if held:

        @pl.when(pl.program_id(0) == 0)
        def fill():
            gather_columns(starts, depths, attns[-1], held[0])

    total = None
    at = 0
    for index, pieces in enumerate(parts):
        columns = held[0] if held and index == count - 1 else attns[index]
        term = times_pieces(columns, weights[at : at + pieces])
        total = term if total is None else total + term
        at += pieces
    out_ref[...] = total.astype(out_ref.dtype)


def outward(attn, stacks, columns, starts=None, depths=()):
    rows = attn.shape[0]
    inner = attn.shape[1] // len(stacks)
    tile = min(1024, columns)
    pieces = [(piece, first // tile) for stack, first in stacks for piece in stack]
    scratch = [] if starts is None else [pltpu.VMEM((rows, inner), jnp.bfloat16)]

    def inner_of(index):
        return pl.BlockSpec((rows, inner), lambda j, *_: (0, index))

    def tile_of(piece, skip):
        return pl.BlockSpec((piece.shape[0], tile), lambda j, *_: (0, skip + j))

    return pl.pallas_call(
        functools.partial(
            outward_kernel, parts=tuple(len(stack) for stack, unused in stacks), depths=depths
        ),
        out_shape=jax.ShapeDtypeStruct((rows, columns), jnp.bfloat16),
        grid_spec=pltpu.PrefetchScalarGridSpec(
            num_scalar_prefetch=1,
            grid=(columns // tile,),
            in_specs=[inner_of(index) for index in range(len(stacks))]
            + [tile_of(*piece) for piece in pieces],
            out_specs=pl.BlockSpec((rows, tile), lambda j, *_: (0, j)),
            scratch_shapes=scratch,
        ),
        compiler_params=parameters(),
        cost_estimate=pl.CostEstimate(
            flops=2 * rows * columns * attn.shape[1],
            bytes_accessed=2 * (columns * (rows + attn.shape[1]) + attn.size),
            transcendentals=0,
        ),
        name="outward",
    )(
        jnp.zeros((1,), jnp.int32) if starts is None else starts,
        *[attn for unused in stacks],
        *[piece for piece, unused in pieces],
    )


def rotation(positions):
    half = HD // 2
    freqs = 500000.0 ** (-jnp.arange(half, dtype=jnp.float32) * 2.0 / HD)
    angles = positions.astype(jnp.float32)[:, None] * freqs[None, :]
    cosine, sine = jnp.cos(angles), jnp.sin(angles)
    return jnp.concatenate([cosine, cosine], axis=1), jnp.concatenate([-sine, sine], axis=1)


def table_and_bounds(behind, first, place):
    rows = behind.shape[0]
    table = jnp.stack([behind, first, place], axis=1).astype(jnp.int32)
    table = jnp.concatenate([table, jnp.zeros((rows, HD - 3), jnp.int32)], axis=1)

    def blocks(array):
        return array.reshape(-1, ROWS)

    bounds = jnp.stack(
        [
            blocks(behind).min(axis=1),
            blocks(behind).max(axis=1),
            blocks(first).min(axis=1),
            blocks(place).max(axis=1),
        ],
        axis=1,
    )
    return table, bounds.reshape(-1).astype(jnp.int32)


def normalize(x_rows, norm_gain):
    wide = x_rows.astype(jnp.float32)
    variance = jnp.mean(wide * wide, axis=-1, keepdims=True) + 1e-05
    return (wide * lax.rsqrt(variance) * norm_gain).astype(jnp.bfloat16)


def first_of_request(request_ids, wanted, count):
    labels = jnp.arange(count, dtype=jnp.int32)
    counts = jnp.sum((request_ids[:, None] == labels[None, :]).astype(jnp.int32), axis=0)
    starts = jnp.cumsum(counts) - counts
    match = wanted[:, None] == labels[None, :]
    return jnp.sum(jnp.where(match, starts[None, :], 0), axis=1)


def logical_pages(page_table, physical):
    labels = jnp.arange(page_table.shape[0], dtype=jnp.int32)
    match = page_table[None, :] == physical[:, None]
    return jnp.sum(jnp.where(match, labels[None, :], 0), axis=1)


def join_pair(lower, mine, peer):
    return jnp.where(
        lower, jnp.concatenate([mine, peer], axis=2), jnp.concatenate([peer, mine], axis=2)
    )


def swapped(block, axis, apart):
    route = [(i, i ^ 1 << apart) for i in range(lax.axis_size(axis))]
    return lax.ppermute(block, axis, route)


def shifted(block, axis, distance):
    route = [(i, i + distance) for i in range(lax.axis_size(axis) - distance)]
    return lax.ppermute(block, axis, route)


def by_heads(x_rows, norm_gain, w_query, w_keyval, w_out, prefix_cache, page_table, request_ids):
    tp_size = lax.axis_size("tp")
    grp_size = lax.axis_size("grp")
    tp_index = lax.axis_index("tp")
    grp_index = lax.axis_index("grp")
    tok_group = x_rows.shape[0] * tp_size
    kv_cols = w_keyval.shape[2]
    kv_need = max(HD, HD * KVH // tp_size)
    kv_heads = kv_need // HD
    pages_dev, page_len = prefix_cache.shape[:2]
    prefix_len = pages_dev * grp_size * page_len
    pair_bits = (kv_need // kv_cols).bit_length() - 1

    normed = normalize(x_rows, norm_gain)
    tokens = lax.all_gather(normed, "tp", axis=0, tiled=True)
    group_start = grp_index * tok_group
    token_index = group_start + jnp.arange(tok_group, dtype=jnp.int32)
    own_seg = lax.dynamic_slice_in_dim(request_ids, group_start, tok_group, 0)
    own_first = first_of_request(request_ids, own_seg, 2 * grp_size)
    own_pos = prefix_len + token_index - own_first
    cosine, sine = rotation(own_pos)
    given = [(tokens, cosine, sine)]
    queries = project(given, [w_query], w_query.shape[1])
    kv_weight = w_keyval.reshape(w_keyval.shape[0], 2 * kv_cols)
    cache = prefix_cache.reshape(pages_dev * page_len, 2, kv_cols)
    if pair_bits == 0:
        own = project(given, [kv_weight], kv_cols)
    else:
        keyval = jnp.dot(tokens, kv_weight, preferred_element_type=jnp.float32)
        keyval = keyval.astype(jnp.bfloat16).reshape(tok_group, 2, kv_cols)
        for bit_num in range(pair_bits):
            lower = tp_index >> bit_num & 1 == 0
            keyval = join_pair(lower, keyval, swapped(keyval, "tp", bit_num))
            cache = join_pair(lower, cache, swapped(cache, "tp", bit_num))
        keys = keyval[:, 0].astype(jnp.float32).reshape(tok_group, -1, HD)
        keys = keys * cosine[:, None] + jnp.roll(keys, HD // 2, axis=2) * sine[:, None]
        keys = keys.reshape(tok_group, kv_need).astype(jnp.bfloat16)
        own = jnp.concatenate([keys, keyval[:, 1]], axis=1)
    before = shifted(own, "grp", 1)
    cache = cache.reshape(pages_dev * page_len, 2 * kv_need)
    prefix = lax.all_gather(cache, "grp", axis=0, tiled=True)
    place = tok_group + jnp.arange(tok_group, dtype=jnp.int32)
    first = own_first - group_start + tok_group
    first = jnp.maximum(jnp.maximum(first, place - prefix_len + 1), 0)
    info = table_and_bounds(own_pos - prefix_len, first, place)
    physical = jnp.arange(page_table.shape[0], dtype=jnp.int32)
    targets = logical_pages(page_table, physical) * page_len
    state = attend_prefix(
        queries, info, [(prefix, 0)], targets, page_len, prefix_len, kv_heads
    )
    attn = attend_suffix(
        [(queries, state, 0, 0, [(before, tok_group, 0), (own, tok_group, 0)])],
        info,
        jnp.array([0, tok_group], jnp.int32),
        kv_heads,
        tok_group,
    )
    return lax.psum_scatter(
        outward(attn, [([w_out], 0)], w_out.shape[1]), "tp", scatter_dimension=0, tiled=True
    )


def by_pairs(x_rows, norm_gain, w_query, w_keyval, w_out, prefix_cache, page_table, request_ids):
    grp_size = lax.axis_size("grp")
    tp_size = lax.axis_size("tp")
    grp_index = lax.axis_index("grp")
    tp_index = lax.axis_index("tp")
    rows, width = x_rows.shape
    kv_cols = w_keyval.shape[2]
    kv_heads = kv_cols // HD
    query_cols = w_query.shape[1]
    pages_dev, page_len = prefix_cache.shape[:2]
    prefix_len = pages_dev * grp_size * page_len
    half = 2 * rows
    sync = lax.optimization_barrier

    def across(block, distance):
        return lax.ppermute(block, "tp", [(i, i ^ distance) for i in range(tp_size)])

    def within(block, even, odd):
        route = [(i, i ^ (odd if i % 2 else even)) for i in range(grp_size)]
        return lax.ppermute(block, "grp", route)

    def swap_first(block):
        return within(block, 2, 4)

    def swap_second(pair):
        return within(pair, 4, 2)

    def swap_core(four):
        return within(four, 1, 1)

    def under(*blocks):
        return jnp.concatenate(blocks, axis=0)

    def share_of(weight):
        part = weight.shape[0] // grp_size
        return lax.dynamic_slice_in_dim(weight, grp_index * part, part, 0)

    def later(block, by):
        route = []
        for place in range(2 * grp_size - by):
            target = place + by
            for side in range(2):
                source_id = place // 2 * tp_size + place % 2 * 2 + side
                target_id = target // 2 * tp_size + target % 2 * 2 + side
                route.append((source_id, target_id))
        return lax.ppermute(block, ("grp", "tp"), route)

    odd = grp_index % 2
    first_hop, second_hop = 2 + 2 * odd, 4 - 2 * odd
    hops = [0, first_hop, second_hop, 6, 1, 1 ^ second_hop, 1 ^ first_hop, 7]
    order = grp_index ^ jnp.stack([jnp.int32(hop) for hop in hops])
    units = width // grp_size // HD
    part = units // 4
    keyval_starts, keyval_depths = order * units, (units * HD,) * grp_size
    query_starts = jnp.concatenate([order * units, order * units + part])
    query_depths = (part * HD,) * grp_size + ((units - part) * HD,) * grp_size
    out_depth = w_out.shape[0] // grp_size
    out_starts, out_depths = order * (out_depth // HD), (out_depth,) * grp_size
    half_start = grp_index * rows * tp_size + tp_index // 2 * half

    def rows_of(plane):
        place = 2 * half + plane % 2 * rows + jnp.arange(rows, dtype=jnp.int32)
        index = half_start - 2 * half + place
        segments = lax.dynamic_slice_in_dim(request_ids, half_start + plane % 2 * rows, rows, 0)
        return index, place, segments

    index, place, segments = [
        under(*pair) for pair in zip(rows_of(tp_index), rows_of(tp_index ^ 1))
    ]

    middle = rows // 2
    normed_a = normalize(x_rows[:middle], norm_gain)
    peer_a = across(normed_a, 1)
    normed_a, w_keyval, w_query, late_gain = sync((normed_a, w_keyval, w_query, norm_gain))
    far_keyval = across(share_of(w_keyval).reshape(width // grp_size, 2 * kv_cols), 2)
    query_share = share_of(w_query)
    query_a, query_b = query_share[: part * HD], query_share[part * HD :]
    far_a = across(query_a, 2)
    normed_b = normalize(x_rows[middle:], late_gain)
    near_cache = prefix_cache.reshape(pages_dev * page_len, 2 * kv_cols)
    far_cache = across(near_cache, 2)
    cache_near = lax.all_gather(near_cache, "grp", axis=0, tiled=True)
    start = first_of_request(request_ids, segments, 2 * grp_size)
    first = start - half_start + 2 * half
    first = jnp.maximum(jnp.maximum(first, place - prefix_len + 1), 0)
    cosine, sine = rotation(prefix_len + index - start)
    table, bounds = table_and_bounds(index - start, first, place)
    near_keyval = w_keyval.reshape(width, 2 * kv_cols)
    physical = jnp.arange(page_table.shape[0], dtype=jnp.int32)
    page_targets = logical_pages(page_table, physical) * page_len
    low = tp_index % 2 * rows
    targets = jnp.stack(
        [base + side for base in (0, half, 2 * half) for side in (low, rows - low)]
    ).astype(jnp.int32)
    held = (far_keyval, far_a, peer_a, query_b, far_cache, near_keyval, normed_a, normed_b, cache_near)
    held, cosine, sine, table, bounds = sync((held, cosine, sine, table, bounds))
    far_keyval, far_a, peer_a, query_b, far_cache, near_keyval, normed_a, normed_b, cache_near = held

    keyval_pair = under(far_keyval, swap_first(far_keyval))
    pair_a = under(far_a, swap_first(far_a))
    far_b = across(query_b, 2)
    cache_far = lax.all_gather(far_cache, "grp", axis=0, tiled=True)
    peer_b = across(normed_b, 1)
    out_share = share_of(w_out)
    cut = w_out.shape[1] // 4 * 3
    out_a, out_b = out_share[:, :cut], out_share[:, cut:]
    keyval_pair, pair_a, far_b, peer_b, normed_b, out_a, out_b, cache_far = sync(
        (keyval_pair, pair_a, far_b, peer_b, normed_b, out_a, out_b, cache_far)
    )

    keyval_four = under(keyval_pair, swap_second(keyval_pair))
    four_a = under(pair_a, swap_second(pair_a))
    pair_b = under(far_b, swap_first(far_b))
    out_a = across(out_a, 2)
    tokens = under(normed_a, normed_b, peer_a, peer_b)
    given = [(tokens, cosine, sine)]
    near_kv = project(given, [near_keyval], kv_cols)
    near_q = project(given, [w_query], query_cols)
    keyval_four, four_a, pair_b, tokens, out_a, out_b, near_kv, near_q = sync(
        (keyval_four, four_a, pair_b, tokens, out_a, out_b, near_kv, near_q)
    )

    keyval_others = swap_core(keyval_four)
    others_a = swap_core(four_a)
    second_b = swap_second(pair_b)
    near_two, near_one = later(near_kv, 2), later(near_kv, 1)

    own_info, peer_info = (table[:rows], bounds[:4]), (table[rows:], bounds[4:])

    def prefix_of(queries, info, cache, at=0):
        return attend_prefix(
            queries, info, [(cache, 0)], page_targets, page_len, prefix_len, kv_heads, at
        )

    near_state = prefix_of(near_q, (table, bounds), cache_near)
    keyval_others, others_a, second_b, near_two, near_one, near_state, tokens, out_a, out_b = sync(
        (keyval_others, others_a, second_b, near_two, near_one, near_state, tokens, out_a, out_b)
    )

    given = [(tokens, cosine, sine)]
    others_b = [swap_core(pair_b), swap_core(second_b)]
    out_pair_a = under(out_a, swap_first(out_a))
    out_b = across(out_b, 2)
    far_kv = project(given, [keyval_four, keyval_others], kv_cols, keyval_starts, keyval_depths)
    others_b, out_pair_a, out_b, far_kv, tokens = sync(
        (others_b, out_pair_a, out_b, far_kv, tokens)
    )

    far_two, far_one = later(far_kv, 2), later(far_kv, 1)
    out_second_a = swap_second(out_pair_a)
    out_pair_b = under(out_b, swap_first(out_b))
    given = [(tokens, cosine, sine)]
    far_weights = [four_a, others_a, pair_b, second_b, *others_b]
    far_q = project(given, far_weights, query_cols, query_starts, query_depths)
    peer_state = prefix_of(far_q, peer_info, cache_far, 1)
    far_two, far_one, out_second_a, out_pair_b, peer_state, far_q = sync(
        (far_two, far_one, out_second_a, out_pair_b, peer_state, far_q)
    )

    def suffix_of(far_state, info, block):
        def parts_of(*arrays):
            return [(array, rows, index) for array in arrays for index in range(2)]

        near = (near_q, near_state, block, block, parts_of(near_two, far_one, near_kv))
        far = (far_q, far_state, block, 0, parts_of(far_two, near_one, far_kv))
        return attend_suffix([near, far], info, targets, kv_heads, tp_size * rows)

    out_others_a = [swap_core(out_pair_a), swap_core(out_second_a)]
    out_second_b = swap_second(out_pair_b)
    peer_attn = suffix_of(peer_state, peer_info, 1)
    out_others_a, out_second_b, peer_attn = sync((out_others_a, out_second_b, peer_attn))

    weights_a = [out_pair_a, out_second_a, *out_others_a]
    rest = w_out.shape[1] - cut
    piece = cut // 3

    def output_of(attn, weights, skip, at, columns):
        stacks = [([w_out], skip + at), (weights, at)]
        return outward(attn, stacks, columns, out_starts, out_depths)

    out_others_b = [swap_core(out_pair_b), swap_core(out_second_b)]
    sent = [output_of(peer_attn, weights_a, 0, 0, piece)]
    peer_attn = sync((peer_attn, sent[0]))[0]
    sent.append(output_of(peer_attn, weights_a, 0, piece, cut - piece))
    out_others_b, peer_attn = sync((out_others_b, sync((peer_attn, sent[1]))[0]))
    weights_b = [out_pair_b, out_second_b, *out_others_b]
    sent.append(output_of(peer_attn, weights_b, cut, 0, rest))
    received = [across(block, 1) for block in sent]
    own_info = (own_info[0], sync((own_info[1], sent[2]))[0])
    own_state = prefix_of(far_q, own_info, cache_far)
    own_attn = suffix_of(own_state, own_info, 0)
    kept_a = output_of(own_attn, weights_a, 0, 0, cut)
    kept_b = output_of(own_attn, weights_b, cut, 0, rest)
    kept = [kept_a[:, :piece], kept_a[:, piece:], kept_b]
    sums = [
        (mine.astype(jnp.float32) + theirs.astype(jnp.float32)).astype(jnp.bfloat16)
        for mine, theirs in zip(kept, received)
    ]
    return jnp.concatenate(sums, axis=1)


def solution(mesh):
    pairs = mesh.shape["tp"] == 4 and mesh.shape["grp"] == 8
    placed = (
        P(("grp", "tp"), None),
        P(),
        P(None, "tp"),
        P(None, None, "tp"),
        P("tp", None),
        P("grp", None, None, "tp"),
        P(),
        P(),
    )
    return jax.shard_map(
        by_pairs if pairs else by_heads,
        mesh=mesh,
        in_specs=placed,
        out_specs=P(("grp", "tp"), None),
        check_vma=False,
    )
```
